512 devices in a mesh: dp: 64 (over z, x_hi, core), head: 8 (over x_lo, y).
Axes of the slice: x: 4 (x_hi: 2, x_lo: 2; x = x_hi * 2 + x_lo), y: 4, z: 16, core: 2. Of those that a mesh axis runs over, the one named last changes fastest.
Arguments:
- queries: bfloat16 [16384, 8192], P('dp', 'head'), may hold values from -8 to 8
- resp_keys: bfloat16 [16384, 1024], P('dp', 'head'), may hold values from -6 to 6
- resp_values: bfloat16 [16384, 1024], P('dp', 'head'), may hold values from -6 to 6
- out_grad: bfloat16 [16384, 8192], P('dp', 'head'), may hold values from -72 to 72
- prefix_keys: bfloat16 [65536, 1024], P(('dp', 'head')), may hold values from -8 to 8, as said below
- prefix_values: bfloat16 [65536, 1024], P(('dp', 'head')), may hold values from -6 to 6
- resp_slot: int32 [16384], P('dp'), may hold values from 0 to 4, as said below
- prefix_len: int32 [16], replicated, may hold values from 512 to 1024, as said below
- prefix_owner: int32 [16], replicated, may hold values from 0 to 3
Outputs:
- query_grad: bfloat16 [16384, 8192], P('dp', 'head')
- resp_key_grad: bfloat16 [16384, 1024], P('dp', 'head')
- resp_value_grad: bfloat16 [16384, 1024], P('dp', 'head')
- prefix_key_grad: bfloat16 [65536, 1024], P(('dp', 'head'))
- prefix_value_grad: bfloat16 [65536, 1024], P(('dp', 'head'))
The draws below stay inside these ranges and needn't reach their ends.
Inputs may be any that keep to these rules, and one draw needn't show every extreme that they name: `resp_slot`: in each block of 4 devices, responses 0 to 3 of the block's prompt lie in this order, each a run of 96 to 256 rows on one device, starting where the previous ended or at the first row of the next device; 4 marks empty rows. In every draw some device is filled by one response and some rows are empty. `prefix_len`: some prompt's prefix has exactly 1024 positions. `prefix_keys`: only the slots of the devices named by prefix_owner are read.
All inputs are finite; a program needn't handle non-finite values.
Results may differ from the reference program's by a relative error of at most 0.035.
Values may be sent and summed in bfloat16 or wider, within the bound.
No kernel may reach another device: no remote copies, remote signals or barrier semaphores. Data moves between devices by JAX's collectives and lax.ppermute only.
A program may use at most 64 MiB of HBM per device.

```python
import math
import jax
import jax.numpy as jnp
from jax import lax

HD = 128
QH = 64
KVH = 8
BLOCK = 4
R_DEV = 256
GROUP = 8
PRE_MAX = 1024
PROMPTS = 16
ROWS = 16384
PRE_ROWS = 65536
N_DP = 64


def draw_queries(key, part):
    key = jax.random.fold_in(key, 3)
    second = jax.random.fold_in(key, 1)
    values = jax.random.normal(second, (ROWS, QH * HD), jnp.float32)
    return jnp.clip(values, -8.0, 8.0).astype(jnp.bfloat16)


def draw_prefix_keys(key, part):
    key = jax.random.fold_in(key, 5)
    values = jax.random.normal(key, (PRE_ROWS, KVH * HD), jnp.float32)
    return jnp.clip(values, -8.0, 8.0).astype(jnp.bfloat16)


def draw_resp_slot(key, part):
    key = jax.random.fold_in(key, 7)
    first, second = jax.random.split(key, 2)
    shortest = R_DEV * 3 // 8
    lengths = jax.random.randint(first, (PROMPTS, BLOCK), shortest, R_DEV + 1)
    picked = jax.random.randint(second, (), 0, PROMPTS)
    prompt_rows = jnp.arange(PROMPTS, dtype=jnp.int32)[:, None]
    resp_cols = jnp.arange(BLOCK, dtype=jnp.int32)[None, :]
    lengths = jnp.where(jnp.logical_and(prompt_rows == picked, resp_cols == 0), R_DEV, lengths)
    lengths = jnp.where(jnp.logical_and(prompt_rows == picked, resp_cols == 1), shortest, lengths)
    device_at = jnp.zeros((PROMPTS,), jnp.int32)
    used_rows = jnp.zeros((PROMPTS,), jnp.int32)
    place = jnp.arange(BLOCK, dtype=jnp.int32)[None, :, None]
    offset = jnp.arange(R_DEV, dtype=jnp.int32)[None, None, :]
    slots = jnp.full((PROMPTS, BLOCK, R_DEV), BLOCK, jnp.int32)
    for resp_index in range(BLOCK):
        length = lengths[:, resp_index]
        moving = used_rows + length > R_DEV
        device_at = device_at + moving.astype(jnp.int32)
        used_rows = jnp.where(moving, 0, used_rows)
        inside = jnp.logical_and(place == device_at[:, None, None], offset >= used_rows[:, None, None])
        inside = jnp.logical_and(inside, offset < (used_rows + length)[:, None, None])
        slots = jnp.where(inside, resp_index, slots)
        used_rows = used_rows + length
    return slots.reshape(PROMPTS * BLOCK * R_DEV)


def draw_prefix_len(key, part):
    key = jax.random.fold_in(key, 9)
    first, second = jax.random.split(key, 2)
    lengths = jax.random.randint(first, (PROMPTS,), PRE_MAX // 2, PRE_MAX + 1)
    picked = jax.random.randint(second, (), 0, PROMPTS)
    return jnp.where(jnp.arange(PROMPTS, dtype=jnp.int32) == picked, PRE_MAX, lengths)


def plant(drawn, rng, least, high):
    spot = [jax.random.randint(jax.random.fold_in(rng, axis), (), 0, length) for axis, length in enumerate(drawn.shape)]
    main_axis = drawn.shape.index(max(drawn.shape))
    beside = spot[:main_axis] + [(spot[main_axis] + 1) % drawn.shape[main_axis]] + spot[main_axis + 1:]
    return drawn.at[tuple(spot)].set(least).at[tuple(beside)].set(high)


def steps_of(rng, shape, cuts, least, largest):
    loudness, own = 1.0, jax.random.fold_in(rng, 6)
    for dim, shards_of in cuts:
        heights = jnp.exp(jax.random.uniform(jax.random.fold_in(own, dim), (shards_of,), jnp.float32, least / len(cuts), largest / len(cuts)))
        loudness = loudness * jnp.repeat(heights, shape[dim] // shards_of).reshape([-1 if axis == dim else 1 for axis in range(len(shape))])
    return loudness


def centred(own_key, extent, deviation, bound, pieces=(), held_as=jnp.bfloat16):
    drawn = jax.random.normal(own_key, extent, jnp.float32) * deviation
    if len(pieces) > 0:
        drawn = steps_of(own_key, extent, pieces, -0.22, 0.18) * drawn
    return jnp.clip(drawn, min=-bound, max=bound).astype(held_as)


def setup_inputs(seed: int = 0) -> dict:
    key_list = jax.random.split(jax.random.key(seed), 10)
    return {
        "queries": draw_queries(jax.random.fold_in(key_list[9], 71), 0),
        "resp_keys": centred(key_list[1], (ROWS, KVH * HD), 1.0, 6.0, ((0, 64), (1, 8))),
        "resp_values": centred(key_list[2], (ROWS, KVH * HD), 1.0, 6.0, ((0, 64), (1, 8))),
        "out_grad": centred(key_list[3], (ROWS, QH * HD), 12.0, 72.0, ((0, 64), (1, 8))),
        "prefix_keys": draw_prefix_keys(jax.random.fold_in(key_list[9], 71), 0),
        "prefix_values": centred(key_list[5], (PRE_ROWS, KVH * HD), 1.0, 6.0, ((0, 512),)),
        "resp_slot": draw_resp_slot(jax.random.fold_in(key_list[9], 71), 0),
        "prefix_len": draw_prefix_len(jax.random.fold_in(key_list[9], 71), 0),
        "prefix_owner": plant(jax.random.randint(key_list[8], (PROMPTS,), 0, BLOCK), jax.random.fold_in(key_list[8], 1), 0, BLOCK - 1).astype(jnp.int32),
    }


masked_score = -1e+30

def device_grads(query_rows, key_rows, value_rows, grad_rows, slot_rows, pre_keys, pre_values, prefix_count):
    live_rows = slot_rows < BLOCK
    live_weight = live_rows.astype(jnp.float32)
    row_index = jnp.arange(R_DEV, dtype=jnp.int32)
    prefix_seen = jnp.logical_and((jnp.arange(PRE_MAX, dtype=jnp.int32) < prefix_count)[None, :], live_rows[:, None])
    same_resp = jnp.logical_and(slot_rows[:, None] == slot_rows[None, :], row_index[None, :] <= row_index[:, None])
    resp_seen = jnp.logical_and(same_resp, live_rows[:, None])
    visible = jnp.concatenate([prefix_seen, resp_seen], axis=1)
    score_scale = 1.0 / math.sqrt(HD)
    all_keys = jnp.concatenate([pre_keys, key_rows], 0).reshape(PRE_MAX + R_DEV, KVH, HD).astype(jnp.float32)
    all_values = jnp.concatenate([pre_values, value_rows], 0).reshape(PRE_MAX + R_DEV, KVH, HD).astype(jnp.float32)
    query_heads = query_rows.reshape(R_DEV, KVH, GROUP, HD).astype(jnp.float32)
    grad_heads = grad_rows.reshape(R_DEV, KVH, GROUP, HD).astype(jnp.float32)

    def one_head(head_index):
        query_group = query_heads[:, head_index]
        grad_group = grad_heads[:, head_index]
        head_keys = all_keys[:, head_index]
        head_values = all_values[:, head_index]
        scores = jnp.einsum('rgd,kd->grk', query_group, head_keys) * score_scale
        scores = jnp.where(visible[None], scores, masked_score)
        exp_terms = jnp.exp(scores - lax.optimization_barrier(jnp.max(scores, axis=-1, keepdims=True)))
        weights = exp_terms / lax.optimization_barrier(jnp.sum(exp_terms, axis=-1, keepdims=True)) * live_weight[None, :, None]
        weights_low = lax.optimization_barrier(weights.astype(jnp.bfloat16)).astype(jnp.float32)
        attended = jnp.einsum('grk,kd->rgd', weights_low, head_values)
        attended = lax.optimization_barrier(attended.astype(jnp.bfloat16)).astype(jnp.float32)
        out_dot = lax.optimization_barrier(jnp.sum(grad_group * attended, axis=-1))
        grad_weights = jnp.einsum('rgd,kd->grk', grad_group, head_values)
        score_grad = weights * (grad_weights - out_dot.T[:, :, None]) * score_scale
        score_low = lax.optimization_barrier(score_grad.astype(jnp.bfloat16)).astype(jnp.float32)
        query_grad = jnp.einsum('grk,kd->rgd', score_low, head_keys).astype(jnp.bfloat16)
        key_grad = jnp.einsum('grk,rgd->kd', score_low, query_group)
        value_grad = jnp.einsum('grk,rgd->kd', weights_low, grad_group)
        return (query_grad, key_grad, value_grad)
    query_grads, key_grads, value_grads = lax.map(one_head, jnp.arange(KVH, dtype=jnp.int32))
    query_grad = jnp.transpose(query_grads, (1, 0, 2, 3)).reshape(R_DEV, QH * HD)
    key_grad = jnp.transpose(key_grads, (1, 0, 2)).reshape(PRE_MAX + R_DEV, KVH * HD)
    value_grad = jnp.transpose(value_grads, (1, 0, 2)).reshape(PRE_MAX + R_DEV, KVH * HD)
    return (query_grad, key_grad[PRE_MAX:].astype(jnp.bfloat16), value_grad[PRE_MAX:].astype(jnp.bfloat16), key_grad[:PRE_MAX], value_grad[:PRE_MAX])

def reference(queries, resp_keys, resp_values, out_grad, prefix_keys, prefix_values, resp_slot, prefix_len, prefix_owner):
    owner_slot = (jnp.arange(PROMPTS, dtype=jnp.int32) * BLOCK + prefix_owner).astype(jnp.int32)
    query_dev = queries.reshape(N_DP, R_DEV, QH * HD)
    key_dev = resp_keys.reshape(N_DP, R_DEV, KVH * HD)
    value_dev = resp_values.reshape(N_DP, R_DEV, KVH * HD)
    grad_dev = out_grad.reshape(N_DP, R_DEV, QH * HD)
    slot_dev = resp_slot.reshape(N_DP, R_DEV)
    pre_key_slots = prefix_keys.reshape(N_DP, PRE_MAX, KVH * HD)
    pre_value_slots = prefix_values.reshape(N_DP, PRE_MAX, KVH * HD)

    def one_device(device_index):
        prompt_index = device_index // BLOCK
        home_slot = owner_slot[prompt_index]
        return device_grads(query_dev[device_index], key_dev[device_index], value_dev[device_index], grad_dev[device_index], slot_dev[device_index], pre_key_slots[home_slot], pre_value_slots[home_slot], prefix_len[prompt_index])
    query_grad, key_grad, value_grad, pre_key_part, pre_value_part = lax.map(one_device, jnp.arange(N_DP, dtype=jnp.int32))
    block_keys = lax.optimization_barrier(jnp.sum(pre_key_part.reshape(PROMPTS, BLOCK, PRE_MAX, KVH * HD), axis=1)).astype(jnp.bfloat16)
    block_values = lax.optimization_barrier(jnp.sum(pre_value_part.reshape(PROMPTS, BLOCK, PRE_MAX, KVH * HD), axis=1)).astype(jnp.bfloat16)
    key_slots = jnp.zeros((N_DP, PRE_MAX, KVH * HD), jnp.bfloat16).at[owner_slot].set(block_keys)
    value_slots = jnp.zeros((N_DP, PRE_MAX, KVH * HD), jnp.bfloat16).at[owner_slot].set(block_values)
    return (query_grad.reshape(ROWS, QH * HD), key_grad.reshape(ROWS, KVH * HD), value_grad.reshape(ROWS, KVH * HD), key_slots.reshape(PRE_ROWS, KVH * HD), value_slots.reshape(PRE_ROWS, KVH * HD))
```

```python
import math

import jax
import jax.numpy as jnp
from jax import lax
from jax.experimental import pallas as pl
from jax.experimental.pallas import tpu as pltpu
from jax.sharding import PartitionSpec as P

HD = 128
QH = 64
KVH = 8
BLOCK = 4
GROUP = QH // KVH
CHUNK = 256
MASKED = -1e30

F32 = jnp.float32
BF16 = jnp.bfloat16
VMEM = pl.BlockSpec(memory_space=pltpu.VMEM)
SMEM = pl.BlockSpec(memory_space=pltpu.SMEM)
PARAMS = pltpu.CompilerParams(vmem_limit_bytes=48 * 1024 * 1024)


def place():
    index = lax.axis_index("dp")
    return index // BLOCK, (index % BLOCK) // 2, index % 2


def call(kernel, outs, *args, scratch=(), flops=0):
    specs = [SMEM if a.dtype == jnp.int32 and a.ndim == 1 else VMEM for a in args]
    size = sum(math.prod(a.shape) * a.dtype.itemsize for a in list(args) + list(outs))
    return pl.pallas_call(
        kernel,
        out_shape=tuple(outs),
        in_specs=specs,
        out_specs=tuple(VMEM for _ in outs),
        scratch_shapes=list(scratch),
        compiler_params=PARAMS,
        cost_estimate=pl.CostEstimate(flops=flops, bytes_accessed=size, transcendentals=0),
    )(*args)


def struct(shape, dtype):
    return jax.ShapeDtypeStruct(shape, dtype)


def half_kernel(key_ref, value_ref, out_ref):
    _, _, core = place()
    half = out_ref.shape[1]
    rows = pl.ds(pl.multiple_of((1 - core) * half, half), half)
    out_ref[0] = key_ref[rows, :]
    out_ref[1] = value_ref[rows, :]


def spread_kernel(owner_ref, key_ref, value_ref, got_ref, out_ref):
    prompt, _, core = place()
    half = got_ref.shape[1]
    rows = pl.ds(pl.multiple_of(core * half, half), half)
    own = owner_ref[prompt] % 2 == core

    @pl.when(own)
    def _():
        for n, ref in enumerate((key_ref, value_ref)):
            for h in range(KVH):
                block = ref[rows, h * HD : (h + 1) * HD]
                out_ref[h, n] = block
                out_ref[KVH + h, n] = block

    @pl.when(jnp.logical_not(own))
    def _():
        for n in range(2):
            for h in range(KVH):
                block = got_ref[n, :, h * HD : (h + 1) * HD]
                out_ref[h, n] = block
                out_ref[KVH + h, n] = block


def side_kernel(owner_ref, got_ref, out_ref):
    prompt, _, _ = place()
    side = owner_ref[prompt] // 2
    out_ref[...] = got_ref[pl.ds(side * KVH, KVH)]


def attention_kernel(
    len_ref, slot_ref, query_ref, grad_ref, own_ref, other_ref, rkey_ref, rvalue_ref,
    dq_ref, drk_ref, drv_ref, part_ref, send_ref,
    key, value, key_t, query, grad, score, dprod, weight, sgrad, bias, rbias,
):
    prompt, _, core = place()
    count = len_ref[prompt]
    rows = query_ref.shape[0]
    pieces, _, half, _ = own_ref.shape
    pre = pieces * half
    total = 2 * pre + rows
    chunks = total // CHUNK
    scale = 1.0 / math.sqrt(HD)
    log_scale = scale * math.log2(math.e)

    for base, ref in ((0, own_ref), (pre, other_ref)):
        for p in range(pieces):
            key[base + p * half : base + (p + 1) * half] = ref[p, 0]
            value[base + p * half : base + (p + 1) * half] = ref[p, 1]
    key[2 * pre :] = rkey_ref[...]
    value[2 * pre :] = rvalue_ref[...]
    for k in range(chunks):
        cut = slice(k * CHUNK, (k + 1) * CHUNK)
        key_t[:, cut] = key[cut].astype(F32).T.astype(BF16)
    for g in range(GROUP):
        query[g * rows : (g + 1) * rows] = query_ref[:, g * HD : (g + 1) * HD]
        grad[g * rows : (g + 1) * rows] = grad_ref[:, g * HD : (g + 1) * HD]

    column = lax.broadcasted_iota(jnp.int32, (pre, HD), 0)
    for n, which in enumerate((core, 1 - core)):
        position = (column // half) * (2 * half) + which * half + column % half
        bias[n * pre : (n + 1) * pre] = jnp.where(position < count, 0.0, MASKED).astype(F32)
    slot = slot_ref[...].astype(F32)
    slot_row = jnp.broadcast_to(slot, (rows, rows))
    slot_col = slot_row.T
    at_key = lax.broadcasted_iota(jnp.int32, (rows, rows), 0)
    at_row = lax.broadcasted_iota(jnp.int32, (rows, rows), 1)
    seen = jnp.logical_and(slot_row == slot_col, at_key <= at_row)
    rbias[...] = jnp.where(seen, 0.0, MASKED).astype(F32)
    live = jnp.where(slot < BLOCK, 1.0, 0.0).astype(F32)

    def head(g, carry):
        at = pl.ds(pl.multiple_of(g * rows, rows), rows)
        query_g = query[at]
        grad_g = grad[at]
        top = jnp.full((1, rows), -jnp.inf, F32)
        for k in range(chunks):
            cut = slice(k * CHUNK, (k + 1) * CHUNK)
            s = lax.dot_general(key[cut], query_g, (((1,), (1,)), ((), ())), preferred_element_type=F32)
            if k == chunks - 1:
                s = s + rbias[...]
            else:
                b = bias[cut]
                s = s + jnp.concatenate([b, b], axis=1)
            score[cut] = s
            top = jnp.maximum(top, jnp.max(s, axis=0, keepdims=True))
        denom = jnp.zeros((1, rows), F32)
        dot = jnp.zeros((1, rows), F32)
        for k in range(chunks):
            cut = slice(k * CHUNK, (k + 1) * CHUNK)
            e = jnp.exp2((score[cut] - top) * log_scale)
            d = lax.dot_general(value[cut], grad_g, (((1,), (1,)), ((), ())), preferred_element_type=F32)
            denom = denom + jnp.sum(e, axis=0, keepdims=True)
            dot = dot + jnp.sum(e * d, axis=0, keepdims=True)
            score[cut] = e
            dprod[cut] = d
        inverse = live / denom
        dot = dot * inverse
        dq = jnp.zeros((HD, rows), F32)
        for k in range(chunks):
            cut = slice(k * CHUNK, (k + 1) * CHUNK)
            w = score[cut] * inverse
            weight[cut, at] = w.astype(BF16)
            ds = (w * (dprod[cut] - dot)).astype(BF16)
            sgrad[cut, at] = ds
            dq = dq + jnp.dot(key_t[:, cut], ds, preferred_element_type=F32)
        lanes = pl.ds(pl.multiple_of(g * HD, HD), HD)
        dq_ref[:, lanes] = (dq * scale).T.astype(BF16)
        return carry

    lax.fori_loop(0, GROUP, head, 0)

    def grads(k):
        cut = slice(k * CHUNK, (k + 1) * CHUNK)
        dk = jnp.dot(sgrad[cut], query[...], preferred_element_type=F32) * scale
        dv = jnp.dot(weight[cut], grad[...], preferred_element_type=F32)
        return dk, dv

    drk, drv = grads(chunks - 1)
    drk_ref[...] = drk.astype(BF16)
    drv_ref[...] = drv.astype(BF16)
    per = CHUNK // half
    for ref, base in ((part_ref, 0), (send_ref, pre // CHUNK)):
        for k in range(pre // CHUNK):
            dk, dv = grads(base + k)
            for p in range(per):
                ref[k * per + p, 0] = dk[p * half : (p + 1) * half].astype(ref.dtype)
                ref[k * per + p, 1] = dv[p * half : (p + 1) * half].astype(ref.dtype)


def chip_sum_kernel(part_ref, got_ref, out_ref):
    for h in range(KVH):
        block = (part_ref[h] + got_ref[h].astype(F32)).astype(BF16)
        out_ref[h] = block
        out_ref[KVH + h] = block


def prompt_sum_kernel(got_ref, out_ref):
    for n in range(2):
        for h in range(KVH):
            block = got_ref[h, n].astype(F32) + got_ref[KVH + h, n].astype(F32)
            out_ref[n, :, h * HD : (h + 1) * HD] = block.astype(BF16)


def final_kernel(owner_ref, mine_ref, got_ref, dk_ref, dv_ref):
    prompt, side, core = place()
    half = mine_ref.shape[1]
    own = owner_ref[prompt] == side * 2 + core
    mine = pl.ds(pl.multiple_of(core * half, half), half)
    other = pl.ds(pl.multiple_of((1 - core) * half, half), half)

    @pl.when(own)
    def _():
        for n, ref in enumerate((dk_ref, dv_ref)):
            ref[mine, :] = mine_ref[n]
            ref[other, :] = got_ref[n]

    @pl.when(jnp.logical_not(own))
    def _():
        for ref in (dk_ref, dv_ref):
            ref[...] = jnp.zeros_like(ref)


def on_device(
    queries,
    resp_keys,
    resp_values,
    out_grad,
    prefix_keys,
    prefix_values,
    resp_slot,
    prefix_len,
    prefix_owner,
):
    dp, heads = lax.axis_size("dp"), lax.axis_size("head")
    rows = queries.shape[0]
    local, width = prefix_keys.shape
    half = local // 2
    total = local * heads + rows
    swap = [(d, d ^ 1) for d in range(dp)]
    groups = [
        [(base + 2 * side + core) * heads + h for side in range(2) for h in range(heads)]
        for base in range(0, dp, BLOCK)
        for core in range(2)
    ]

    def exchange(block):
        flat = block.reshape(2 * heads, 2 * half, HD)
        flat = lax.all_to_all(flat, ("dp", "head"), 0, 0, axis_index_groups=groups, tiled=True)
        return flat.reshape(block.shape)

    piece = (heads, 2, half, HD)
    (sent,) = call(half_kernel, [struct((2, half, width), BF16)], prefix_keys, prefix_values)
    got = lax.ppermute(sent, "dp", swap)
    (spread,) = call(
        spread_kernel, [struct((2 * heads, 2, half, HD), BF16)], prefix_owner, prefix_keys, prefix_values, got
    )
    arrived = exchange(spread)
    (own,) = call(side_kernel, [struct(piece, BF16)], prefix_owner, arrived)
    other = lax.ppermute(own, "dp", swap)
    dq, drk, drv, part, send = call(
        attention_kernel,
        [
            struct(queries.shape, BF16),
            struct(resp_keys.shape, BF16),
            struct(resp_values.shape, BF16),
            struct(piece, F32),
            struct(piece, BF16),
        ],
        prefix_len,
        resp_slot.reshape(1, rows),
        queries,
        out_grad,
        own,
        other,
        resp_keys,
        resp_values,
        scratch=[
            pltpu.VMEM((total, HD), BF16),
            pltpu.VMEM((total, HD), BF16),
            pltpu.VMEM((HD, total), BF16),
            pltpu.VMEM((GROUP * rows, HD), BF16),
            pltpu.VMEM((GROUP * rows, HD), BF16),
            pltpu.VMEM((total, rows), F32),
            pltpu.VMEM((total, rows), F32),
            pltpu.VMEM((total, GROUP * rows), BF16),
            pltpu.VMEM((total, GROUP * rows), BF16),
            pltpu.VMEM((local * heads, HD), F32),
            pltpu.VMEM((rows, rows), F32),
        ],
        flops=10 * GROUP * rows * total * HD,
    )
    got = lax.ppermute(send, "dp", swap)
    (spread,) = call(chip_sum_kernel, [struct((2 * heads, 2, half, HD), BF16)], part, got)
    arrived = exchange(spread)
    (mine,) = call(prompt_sum_kernel, [struct((2, half, width), BF16)], arrived)
    got = lax.ppermute(mine, "dp", swap)
    dk, dv = call(
        final_kernel,
        [struct(prefix_keys.shape, BF16), struct(prefix_values.shape, BF16)],
        prefix_owner,
        mine,
        got,
    )
    return dq, drk, drv, dk, dv


def solution(mesh):
    placed = (
        P("dp", "head"),
        P("dp", "head"),
        P("dp", "head"),
        P("dp", "head"),
        P(("dp", "head"), None),
        P(("dp", "head"), None),
        P("dp"),
        P(),
        P(),
    )
    return jax.shard_map(
        on_device,
        mesh=mesh,
        in_specs=placed,
        out_specs=(
            P("dp", "head"),
            P("dp", "head"),
            P("dp", "head"),
            P(("dp", "head"), None),
            P(("dp", "head"), None),
        ),
        check_vma=False,
    )
```

```python
import math

import jax
import jax.numpy as jnp
from jax import lax
from jax.experimental import pallas as pl
from jax.experimental.pallas import tpu as pltpu
from jax.sharding import PartitionSpec as P

HD = 128
QH = 64
KVH = 8
BLOCK = 4
GROUP = QH // KVH
CHUNK = 256
MASKED = -1e30

F32 = jnp.float32
BF16 = jnp.bfloat16
VMEM = pl.BlockSpec(memory_space=pltpu.VMEM)
HBM = pl.BlockSpec(memory_space=pltpu.HBM)
PARAMS = pltpu.CompilerParams(vmem_limit_bytes=48 * 1024 * 1024)


def place():
    index = lax.axis_index("dp")
    return index // BLOCK, (index % BLOCK) // 2, index % 2


def owner_of(ref):
    prompt, _, _ = place()
    lane = lax.broadcasted_iota(jnp.int32, ref.shape, 1)
    return jnp.sum(jnp.where(lane == prompt, ref[...], 0).astype(F32)).astype(jnp.int32)


def nt(a, b):
    return lax.dot_general(a, b, (((1,), (1,)), ((), ())), preferred_element_type=F32)


def nn(a, b):
    return jnp.dot(a, b, preferred_element_type=F32)


def call(kernel, outs, *args, specs=None, scratch=(), flops=0):
    size = sum(math.prod(a.shape) * a.dtype.itemsize for a in list(args) + list(outs))
    return pl.pallas_call(
        kernel,
        out_shape=tuple(outs),
        in_specs=specs or [VMEM for _ in args],
        out_specs=tuple(VMEM for _ in outs),
        scratch_shapes=list(scratch),
        compiler_params=PARAMS,
        cost_estimate=pl.CostEstimate(flops=flops, bytes_accessed=size, transcendentals=0),
    )(*args)


def struct(shape, dtype):
    return jax.ShapeDtypeStruct(shape, dtype)


def spread_kernel(key_ref, value_ref, out_ref, sems):
    copies = []
    for n, ref in enumerate((key_ref, value_ref)):
        for h in range(KVH):
            for side in range(2):
                source = ref.at[:, h * HD : (h + 1) * HD]
                target = out_ref.at[side * KVH + h, n]
                copies.append(pltpu.make_async_copy(source, target, sems.at[len(copies)]))
    for copy in copies:
        copy.start()
    for copy in copies:
        copy.wait()


def side_kernel(owner_ref, got_ref, out_ref):
    side = owner_of(owner_ref) // 2

    @pl.when(side == 0)
    def _():
        out_ref[...] = got_ref[:KVH]

    @pl.when(side == 1)
    def _():
        out_ref[...] = got_ref[KVH:]


def prepare_kernel(len_ref, slot_ref, query_ref, grad_ref, query_t, grad_t, bias, rbias):
    rows = query_ref.shape[0]
    for g in range(GROUP):
        at = slice(g * rows, (g + 1) * rows)
        lanes = slice(g * HD, (g + 1) * HD)
        query_t[:, at] = query_ref[:, lanes].T
        grad_t[:, at] = grad_ref[:, lanes].T
    prompt, _, _ = place()
    lane = lax.broadcasted_iota(jnp.int32, len_ref.shape, 1)
    count = jnp.sum(jnp.where(lane == prompt, len_ref[...], 0).astype(F32), axis=1, keepdims=True)
    column = lax.broadcasted_iota(jnp.int32, bias.shape, 0).astype(F32)
    bias[...] = jnp.where(column < count, 0.0, MASKED).astype(F32)
    slot_row = jnp.broadcast_to(slot_ref[...].astype(F32), (rows, rows))
    slot_col = slot_row.T
    at_key = lax.broadcasted_iota(jnp.int32, (rows, rows), 0)
    at_row = lax.broadcasted_iota(jnp.int32, (rows, rows), 1)
    seen = jnp.logical_and(slot_row == slot_col, at_key <= at_row)
    rbias[...] = jnp.where(seen, 0.0, MASKED).astype(F32)


def attention_kernel(
    owner_ref, slot_ref, query, grad, bias, rbias, own_ref, other_ref, rkey_ref, rvalue_ref,
    dq_ref, drk_ref, drv_ref, part_ref,
    key, value, key_t, value_t, query_s, grad_s, score, weight, sgrad, factor,
):
    _, _, core = place()
    rows = slot_ref.shape[1]
    pieces, _, local, _ = own_ref.shape
    pre = pieces * local
    total = pre + rows
    chunks = total // CHUNK
    scale = 1.0 / math.sqrt(HD)
    log_scale = scale * math.log2(math.e)
    live = jnp.where(slot_ref[...] < BLOCK, 1.0, 0.0).astype(F32)

    def take(ref):
        for p in range(pieces):
            key[p * local : (p + 1) * local] = ref[p, 0]
            value[p * local : (p + 1) * local] = ref[p, 1]

    own = owner_of(owner_ref) % 2 == core
    pl.when(own)(lambda: take(own_ref))
    pl.when(jnp.logical_not(own))(lambda: take(other_ref))
    key[pre:] = rkey_ref[...]
    value[pre:] = rvalue_ref[...]

    def cut(k):
        return slice(k * CHUNK, (k + 1) * CHUNK)

    def at(g):
        return slice(g * rows, (g + 1) * rows)

    for k in range(chunks):
        key_t[:, cut(k)] = key[cut(k)].T
        value_t[:HD, cut(k)] = value[cut(k)].T
    value_t[HD:] = jnp.ones((value_t.shape[0] - HD, total), BF16)

    tops, dots = {}, {}

    def scores(g, k):
        s = nn(key[cut(k)], query[:, at(g)])
        if k == chunks - 1:
            s = s + rbias[...]
        else:
            b = bias[cut(k)]
            s = s + jnp.concatenate([b] * (rows // HD), axis=1)
        score[g % 2, cut(k)] = s
        top = jnp.max(s, axis=0, keepdims=True)
        tops[g] = top if k == 0 else jnp.maximum(tops[g], top)

    def weights(g, k):
        weight[cut(k), at(g)] = jnp.exp2((score[g % 2, cut(k)] - tops[g]) * log_scale).astype(BF16)

    def attend(g):
        both = nn(value_t[...], weight[:, at(g)])
        denom = both[HD : HD + 1]
        inverse = live / denom
        dots[g] = jnp.sum(both[:HD] * grad[:, at(g)].astype(F32), axis=0, keepdims=True) / denom
        factor[:, at(g)] = inverse * scale
        query_s[:, at(g)] = (query[:, at(g)].astype(F32) * (inverse * scale)).astype(BF16)
        grad_s[:, at(g)] = (grad[:, at(g)].astype(F32) * inverse).astype(BF16)

    def score_grads(g, k):
        d = nn(value[cut(k)], grad[:, at(g)])
        sgrad[cut(k), at(g)] = weight[cut(k), at(g)] * (d - dots[g]).astype(BF16)

    for t in range(GROUP + 2):
        for k in range(chunks):
            if t < GROUP:
                scores(t, k)
            if 1 <= t <= GROUP:
                weights(t - 1, k)
            if t >= 2:
                score_grads(t - 2, k)
        if 1 <= t <= GROUP:
            attend(t - 1)

    for k in range(chunks):
        dk = nt(query_s[...], sgrad[cut(k)])
        dv = nt(grad_s[...], weight[cut(k)])
        if k == chunks - 1:
            drk_ref[...] = dk.T.astype(BF16)
            drv_ref[...] = dv.T.astype(BF16)
        else:
            for p in range(CHUNK // local):
                for n, d in enumerate((dk, dv)):
                    block = d[:, p * local : (p + 1) * local].T.astype(BF16)
                    part_ref[k * (CHUNK // local) + p, n] = block
                    part_ref[pieces + k * (CHUNK // local) + p, n] = block
    for g in range(GROUP):
        dq = nn(key_t[...], sgrad[:, at(g)]) * factor[:, at(g)]
        dq_ref[:, g * HD : (g + 1) * HD] = dq.T.astype(BF16)


def side_sum_kernel(got_ref, out_ref):
    for n in range(2):
        for h in range(KVH):
            block = got_ref[h, n].astype(F32) + got_ref[KVH + h, n].astype(F32)
            out_ref[n, :, h * HD : (h + 1) * HD] = block.astype(BF16)


def final_kernel(owner_ref, mine_ref, got_ref, dk_ref, dv_ref):
    _, side, core = place()
    own = owner_of(owner_ref) == side * 2 + core

    @pl.when(own)
    def _():
        for n, ref in enumerate((dk_ref, dv_ref)):
            ref[...] = (mine_ref[n].astype(F32) + got_ref[n].astype(F32)).astype(BF16)

    @pl.when(jnp.logical_not(own))
    def _():
        for ref in (dk_ref, dv_ref):
            ref[...] = jnp.zeros_like(ref)


def on_device(
    queries,
    resp_keys,
    resp_values,
    out_grad,
    prefix_keys,
    prefix_values,
    resp_slot,
    prefix_len,
    prefix_owner,
):
    dp, heads = lax.axis_size("dp"), lax.axis_size("head")
    rows = queries.shape[0]
    local, width = prefix_keys.shape
    pre = local * heads
    total = pre + rows
    swap = [(d, d ^ 1) for d in range(dp)]
    groups = [
        [(base + 2 * side + core) * heads + h for side in range(2) for h in range(heads)]
        for base in range(0, dp, BLOCK)
        for core in range(2)
    ]

    def exchange(block):
        flat = block.reshape(2 * heads, 2 * local, HD)
        flat = lax.all_to_all(flat, ("dp", "head"), 0, 0, axis_index_groups=groups, tiled=True)
        return flat.reshape(block.shape)

    owner = prefix_owner.reshape(1, -1)
    slot = resp_slot.reshape(1, rows)
    both = (2 * heads, 2, local, HD)
    (spread,) = call(
        spread_kernel,
        [struct(both, BF16)],
        prefix_keys,
        prefix_values,
        specs=[HBM, HBM],
        scratch=[pltpu.SemaphoreType.DMA((4 * heads,))],
    )
    (own,) = call(side_kernel, [struct((heads, 2, local, HD), BF16)], owner, exchange(spread))
    other = lax.ppermute(own, "dp", swap)
    query_t, grad_t, bias, rbias = call(
        prepare_kernel,
        [
            struct((HD, GROUP * rows), BF16),
            struct((HD, GROUP * rows), BF16),
            struct((pre, HD), F32),
            struct((rows, rows), F32),
        ],
        prefix_len.reshape(1, -1),
        slot,
        queries,
        out_grad,
    )
    dq, drk, drv, part = call(
        attention_kernel,
        [
            struct(queries.shape, BF16),
            struct(resp_keys.shape, BF16),
            struct(resp_values.shape, BF16),
            struct(both, BF16),
        ],
        owner,
        slot,
        query_t,
        grad_t,
        bias,
        rbias,
        own,
        other,
        resp_keys,
        resp_values,
        scratch=[
            pltpu.VMEM((total, HD), BF16),
            pltpu.VMEM((total, HD), BF16),
            pltpu.VMEM((HD, total), BF16),
            pltpu.VMEM((HD + 16, total), BF16),
            pltpu.VMEM((HD, GROUP * rows), BF16),
            pltpu.VMEM((HD, GROUP * rows), BF16),
            pltpu.VMEM((2, total, rows), F32),
            pltpu.VMEM((total, GROUP * rows), BF16),
            pltpu.VMEM((total, GROUP * rows), BF16),
            pltpu.VMEM((1, GROUP * rows), F32),
        ],
        flops=12 * GROUP * rows * total * HD,
    )
    (mine,) = call(side_sum_kernel, [struct((2, local, width), BF16)], exchange(part))
    got = lax.ppermute(mine, "dp", swap)
    dk, dv = call(
        final_kernel,
        [struct(prefix_keys.shape, BF16), struct(prefix_values.shape, BF16)],
        owner,
        mine,
        got,
    )
    return dq, drk, drv, dk, dv


def solution(mesh):
    placed = (
        P("dp", "head"),
        P("dp", "head"),
        P("dp", "head"),
        P("dp", "head"),
        P(("dp", "head"), None),
        P(("dp", "head"), None),
        P("dp"),
        P(),
        P(),
    )
    return jax.shard_map(
        on_device,
        mesh=mesh,
        in_specs=placed,
        out_specs=(
            P("dp", "head"),
            P("dp", "head"),
            P("dp", "head"),
            P(("dp", "head"), None),
            P(("dp", "head"), None),
        ),
        check_vma=False,
    )
```

```python
import math

import jax
import jax.numpy as jnp
from jax import lax
from jax.experimental import pallas as pl
from jax.experimental.pallas import tpu as pltpu
from jax.sharding import PartitionSpec as P

HD = 128
QH = 64
KVH = 8
BLOCK = 4
GROUP = QH // KVH
CHUNK = 256
MASKED = -1e30

F32 = jnp.float32
BF16 = jnp.bfloat16
VMEM = pl.BlockSpec(memory_space=pltpu.VMEM)
HBM = pl.BlockSpec(memory_space=pltpu.HBM)
MIB = 1024 * 1024


def place():
    index = lax.axis_index("dp")
    return index // BLOCK, (index % BLOCK) // 2, index % 2


def nt(a, b):
    return lax.dot_general(a, b, (((1,), (1,)), ((), ())), preferred_element_type=F32)


def nn(a, b):
    return jnp.dot(a, b, preferred_element_type=F32)


def call(kernel, outs, *args, specs=None, scratch=(), flops=0, vmem=32):
    size = sum(math.prod(a.shape) * a.dtype.itemsize for a in list(args) + list(outs))
    return pl.pallas_call(
        kernel,
        out_shape=tuple(outs),
        in_specs=specs or [VMEM for _ in args],
        out_specs=tuple(VMEM for _ in outs),
        scratch_shapes=list(scratch),
        compiler_params=pltpu.CompilerParams(vmem_limit_bytes=vmem * MIB),
        cost_estimate=pl.CostEstimate(flops=flops, bytes_accessed=size, transcendentals=0),
    )(*args)


def struct(shape, dtype):
    return jax.ShapeDtypeStruct(shape, dtype)


def spread_kernel(owner_ref, key_ref, value_ref, out_ref, flag_ref, place_ref, owners, sems):
    copies = [pltpu.make_async_copy(owner_ref, owners, sems.at[0])]
    for n, ref in enumerate((key_ref, value_ref)):
        for h in range(KVH):
            for side in range(2):
                source = ref.at[:, h * HD : (h + 1) * HD]
                target = out_ref.at[side * KVH + h, n]
                copies.append(pltpu.make_async_copy(source, target, sems.at[len(copies)]))
    for copy in copies:
        copy.start()
    copies[0].wait()
    prompt, _, core = place()
    owner = owners[0, prompt]
    flag_ref[...] = jnp.full(flag_ref.shape, (owner % 2 == core).astype(jnp.int32))
    place_ref[...] = jnp.full(place_ref.shape, owner)
    for copy in copies[1:]:
        copy.wait()


def side_kernel(place_ref, got_ref, out_ref):
    side = place_ref[0, 0] // 2

    @pl.when(side == 0)
    def _():
        out_ref[...] = got_ref[:KVH]

    @pl.when(side == 1)
    def _():
        out_ref[...] = got_ref[KVH:]


def prepare_kernel(len_ref, slot_ref, query_ref, grad_ref, query_t, grad_t, bias, rbias):
    rows = query_ref.shape[0]
    for g in range(GROUP):
        at = slice(g * rows, (g + 1) * rows)
        lanes = slice(g * HD, (g + 1) * HD)
        query_t[:, at] = query_ref[:, lanes].T
        grad_t[:, at] = grad_ref[:, lanes].T
    prompt, _, _ = place()
    lane = lax.broadcasted_iota(jnp.int32, len_ref.shape, 1)
    count = jnp.sum(jnp.where(lane == prompt, len_ref[...], 0).astype(F32), axis=1, keepdims=True)
    column = lax.broadcasted_iota(jnp.int32, bias.shape, 0).astype(F32)
    bias[...] = jnp.where(column < count, 0.0, MASKED).astype(F32)
    slot_row = jnp.broadcast_to(slot_ref[...].astype(F32), (rows, rows))
    slot_col = slot_row.T
    at_key = lax.broadcasted_iota(jnp.int32, (rows, rows), 0)
    at_row = lax.broadcasted_iota(jnp.int32, (rows, rows), 1)
    seen = jnp.logical_and(slot_row == slot_col, at_key <= at_row)
    rbias[...] = jnp.where(seen, 0.0, MASKED).astype(F32)


def attention_kernel(
    place_ref, slot_ref, query, grad, bias, rbias, own_ref, other_ref, rkey_ref, rvalue_ref,
    dq_ref, drk_ref, drv_ref, part_ref,
    key, value, key_t, value_t, query_s, grad_s, score, weight, sgrad, factor,
):
    _, _, core = place()
    rows = slot_ref.shape[1]
    pieces, _, local, _ = own_ref.shape
    pre = pieces * local
    total = pre + rows
    chunks = total // CHUNK
    scale = 1.0 / math.sqrt(HD)
    log_scale = scale * math.log2(math.e)
    live = jnp.where(slot_ref[...] < BLOCK, 1.0, 0.0).astype(F32)

    def take(ref):
        for p in range(pieces):
            key[p * local : (p + 1) * local] = ref[p, 0]
            value[p * local : (p + 1) * local] = ref[p, 1]

    own = place_ref[0, 0] % 2 == core
    pl.when(own)(lambda: take(own_ref))
    pl.when(jnp.logical_not(own))(lambda: take(other_ref))
    key[pre:] = rkey_ref[...]
    value[pre:] = rvalue_ref[...]

    def cut(k):
        return slice(k * CHUNK, (k + 1) * CHUNK)

    def at(g):
        return slice(g * rows, (g + 1) * rows)

    for k in range(chunks):
        key_t[:, cut(k)] = key[cut(k)].T
        value_t[:HD, cut(k)] = value[cut(k)].T
    value_t[HD:] = jnp.ones((value_t.shape[0] - HD, total), BF16)

    tops, dots = {}, {}

    def scores(g, k):
        s = nn(key[cut(k)], query[:, at(g)])
        if k == chunks - 1:
            s = s + rbias[...]
        else:
            b = bias[cut(k)]
            s = s + jnp.concatenate([b] * (rows // HD), axis=1)
        score[g % 2, cut(k)] = s
        top = jnp.max(s, axis=0, keepdims=True)
        tops[g] = top if k == 0 else jnp.maximum(tops[g], top)

    def weights(g, k):
        weight[cut(k), at(g)] = jnp.exp2((score[g % 2, cut(k)] - tops[g]) * log_scale).astype(BF16)

    def attend(g):
        both = nn(value_t[...], weight[:, at(g)])
        denom = both[HD : HD + 1]
        inverse = live / denom
        dots[g] = jnp.sum(both[:HD] * grad[:, at(g)].astype(F32), axis=0, keepdims=True) / denom
        factor[:, at(g)] = inverse * scale
        query_s[:, at(g)] = (query[:, at(g)].astype(F32) * (inverse * scale)).astype(BF16)
        grad_s[:, at(g)] = (grad[:, at(g)].astype(F32) * inverse).astype(BF16)

    def score_grads(g, k):
        d = nn(value[cut(k)], grad[:, at(g)])
        sgrad[cut(k), at(g)] = weight[cut(k), at(g)] * (d - dots[g]).astype(BF16)

    for t in range(GROUP + 2):
        for k in range(chunks):
            if t < GROUP:
                scores(t, k)
            if 1 <= t <= GROUP:
                weights(t - 1, k)
            if t >= 2:
                score_grads(t - 2, k)
        if 1 <= t <= GROUP:
            attend(t - 1)

    for k in range(chunks):
        dk = nt(query_s[...], sgrad[cut(k)])
        dv = nt(grad_s[...], weight[cut(k)])
        if k == chunks - 1:
            drk_ref[...] = dk.T.astype(BF16)
            drv_ref[...] = dv.T.astype(BF16)
        else:
            for p in range(CHUNK // local):
                for n, d in enumerate((dk, dv)):
                    block = d[:, p * local : (p + 1) * local].T.astype(BF16)
                    part_ref[k * (CHUNK // local) + p, n] = block
    for g in range(GROUP):
        dq = nn(key_t[...], sgrad[:, at(g)]) * factor[:, at(g)]
        dq_ref[:, g * HD : (g + 1) * HD] = dq.T.astype(BF16)


def chip_sum_kernel(mine_ref, got_ref, out_ref):
    for h in range(KVH):
        block = (mine_ref[h].astype(F32) + got_ref[h].astype(F32)).astype(BF16)
        out_ref[h] = block
        out_ref[KVH + h] = block


def final_kernel(place_ref, got_ref, dk_ref, dv_ref):
    _, side, core = place()
    own = place_ref[0, 0] == side * 2 + core

    @pl.when(own)
    def _():
        for n, ref in enumerate((dk_ref, dv_ref)):
            for h in range(KVH):
                block = got_ref[h, n].astype(F32) + got_ref[KVH + h, n].astype(F32)
                ref[:, h * HD : (h + 1) * HD] = block.astype(BF16)

    @pl.when(jnp.logical_not(own))
    def _():
        for ref in (dk_ref, dv_ref):
            ref[...] = jnp.zeros_like(ref)


def on_device(
    queries,
    resp_keys,
    resp_values,
    out_grad,
    prefix_keys,
    prefix_values,
    resp_slot,
    prefix_len,
    prefix_owner,
):
    dp, heads = lax.axis_size("dp"), lax.axis_size("head")
    rows = queries.shape[0]
    local, width = prefix_keys.shape
    pre = local * heads
    total = pre + rows
    swap = [(d, d ^ 1) for d in range(dp)]
    groups = [
        [(base + 2 * side + core) * heads + h for side in range(2) for h in range(heads)]
        for base in range(0, dp, BLOCK)
        for core in range(2)
    ]

    def exchange(block):
        flat = block.reshape(2 * heads, 2 * local, HD)
        flat = lax.all_to_all(flat, ("dp", "head"), 0, 0, axis_index_groups=groups, tiled=True)
        return flat.reshape(block.shape)

    slot = resp_slot.reshape(1, rows)
    piece = (heads, 2, local, HD)
    both = (2 * heads, 2, local, HD)
    spread, flag, owner = call(
        spread_kernel,
        [struct(both, BF16), struct((1, 1), jnp.int32), struct((1, HD), jnp.int32)],
        prefix_owner.reshape(1, -1),
        prefix_keys,
        prefix_values,
        specs=[HBM, HBM, HBM],
        scratch=[pltpu.SMEM((1, prefix_owner.shape[0]), jnp.int32), pltpu.SemaphoreType.DMA((4 * heads + 1,))],
        vmem=60,
    )
    active = flag[0, 0] == 1
    arrived = lax.cond(active, exchange, lambda block: block, spread)
    (own,) = call(side_kernel, [struct(piece, BF16)], owner, arrived)
    other = lax.ppermute(own, "dp", swap)
    query_t, grad_t, bias, rbias = call(
        prepare_kernel,
        [
            struct((HD, GROUP * rows), BF16),
            struct((HD, GROUP * rows), BF16),
            struct((pre, HD), F32),
            struct((rows, rows), F32),
        ],
        prefix_len.reshape(1, -1),
        slot,
        queries,
        out_grad,
    )
    dq, drk, drv, part = call(
        attention_kernel,
        [
            struct(queries.shape, BF16),
            struct(resp_keys.shape, BF16),
            struct(resp_values.shape, BF16),
            struct(piece, BF16),
        ],
        owner,
        slot,
        query_t,
        grad_t,
        bias,
        rbias,
        own,
        other,
        resp_keys,
        resp_values,
        scratch=[
            pltpu.VMEM((total, HD), BF16),
            pltpu.VMEM((total, HD), BF16),
            pltpu.VMEM((HD, total), BF16),
            pltpu.VMEM((HD + 16, total), BF16),
            pltpu.VMEM((HD, GROUP * rows), BF16),
            pltpu.VMEM((HD, GROUP * rows), BF16),
            pltpu.VMEM((2, total, rows), F32),
            pltpu.VMEM((total, GROUP * rows), BF16),
            pltpu.VMEM((total, GROUP * rows), BF16),
            pltpu.VMEM((1, GROUP * rows), F32),
        ],
        flops=12 * GROUP * rows * total * HD,
    )
    got = lax.ppermute(part, "dp", swap)
    (spread,) = call(chip_sum_kernel, [struct(both, BF16)], part, got)
    arrived = lax.cond(active, exchange, lambda block: block, spread)
    dk, dv = call(
        final_kernel,
        [struct(prefix_keys.shape, BF16), struct(prefix_values.shape, BF16)],
        owner,
        arrived,
    )
    return dq, drk, drv, dk, dv


def solution(mesh):
    placed = (
        P("dp", "head"),
        P("dp", "head"),
        P("dp", "head"),
        P("dp", "head"),
        P(("dp", "head"), None),
        P(("dp", "head"), None),
        P("dp"),
        P(),
        P(),
    )
    return jax.shard_map(
        on_device,
        mesh=mesh,
        in_specs=placed,
        out_specs=(
            P("dp", "head"),
            P("dp", "head"),
            P("dp", "head"),
            P(("dp", "head"), None),
            P(("dp", "head"), None),
        ),
        check_vma=False,
    )
```

```python
import math

import jax
import jax.numpy as jnp
from jax import lax
from jax.experimental import pallas as pl
from jax.experimental.pallas import tpu as pltpu
from jax.sharding import PartitionSpec as P

HD = 128
QH = 64
KVH = 8
BLOCK = 4
GROUP = QH // KVH
CHUNK = 256
MASKED = -1e30

F32 = jnp.float32
BF16 = jnp.bfloat16
VMEM = pl.BlockSpec(memory_space=pltpu.VMEM)
HBM = pl.BlockSpec(memory_space=pltpu.HBM)
MIB = 1024 * 1024
PARTS = 4


def place():
    index = lax.axis_index("dp")
    return index // BLOCK, (index % BLOCK) // 2, index % 2


def nt(a, b):
    return lax.dot_general(a, b, (((1,), (1,)), ((), ())), preferred_element_type=F32)


def nn(a, b):
    return jnp.dot(a, b, preferred_element_type=F32)


def call(kernel, outs, *args, specs=None, scratch=(), flops=0, vmem=32):
    size = sum(math.prod(a.shape) * a.dtype.itemsize for a in list(args) + list(outs))
    return pl.pallas_call(
        kernel,
        out_shape=tuple(outs),
        in_specs=specs or [VMEM for _ in args],
        out_specs=tuple(VMEM for _ in outs),
        scratch_shapes=list(scratch),
        compiler_params=pltpu.CompilerParams(vmem_limit_bytes=vmem * MIB),
        cost_estimate=pl.CostEstimate(flops=flops, bytes_accessed=size, transcendentals=0),
    )(*args)


def struct(shape, dtype):
    return jax.ShapeDtypeStruct(shape, dtype)


def spread_kernel(owner_ref, key_ref, value_ref, out_ref, flag_ref, place_ref, slots, owners, sems):
    first = pltpu.make_async_copy(owner_ref, owners, sems.at[0])
    first.start()
    copies = []
    for n, ref in enumerate((key_ref, value_ref)):
        for part in range(PARTS):
            rows = slice(part * HD // PARTS, (part + 1) * HD // PARTS)
            copies.append(pltpu.make_async_copy(ref.at[rows, :], slots.at[n, rows, :], sems.at[len(copies) + 1]))
    for copy in copies:
        copy.start()
    first.wait()
    prompt, side, core = place()
    owner = owners[0, prompt]
    flag_ref[...] = jnp.full(flag_ref.shape, (owner % 2 == core).astype(jnp.int32))
    place_ref[...] = jnp.full(place_ref.shape, owner)

    @pl.when(owner // 2 != side)
    def _():
        out_ref[...] = jnp.zeros_like(out_ref)

    for n in range(2):
        for copy in copies[n * PARTS : (n + 1) * PARTS]:
            copy.wait()

        @pl.when(owner // 2 == side)
        def _():
            for h in range(KVH):
                block = slots[n, :, h * HD : (h + 1) * HD]
                out_ref[h, n] = block
                out_ref[KVH + h, n] = block


def side_kernel(got_ref, out_ref):
    out_ref[...] = got_ref[:KVH] + got_ref[KVH:]


def prepare_kernel(len_ref, slot_ref, query_ref, grad_ref, query_t, grad_t, bias, rbias):
    rows = query_ref.shape[0]
    for g in range(GROUP):
        at = slice(g * rows, (g + 1) * rows)
        lanes = slice(g * HD, (g + 1) * HD)
        query_t[:, at] = query_ref[:, lanes].T
        grad_t[:, at] = grad_ref[:, lanes].T
    prompt, _, _ = place()
    lane = lax.broadcasted_iota(jnp.int32, len_ref.shape, 1)
    count = jnp.sum(jnp.where(lane == prompt, len_ref[...], 0).astype(F32), axis=1, keepdims=True)
    column = lax.broadcasted_iota(jnp.int32, bias.shape, 0).astype(F32)
    bias[...] = jnp.where(column < count, 0.0, MASKED).astype(F32)
    slot_row = jnp.broadcast_to(slot_ref[...].astype(F32), (rows, rows))
    slot_col = slot_row.T
    at_key = lax.broadcasted_iota(jnp.int32, (rows, rows), 0)
    at_row = lax.broadcasted_iota(jnp.int32, (rows, rows), 1)
    seen = jnp.logical_and(slot_row == slot_col, at_key <= at_row)
    rbias[...] = jnp.where(seen, 0.0, MASKED).astype(F32)


def attention_kernel(
    slot_ref, query, grad, bias, rbias, own_ref, other_ref, rkey_ref, rvalue_ref,
    part_ref, weight, sgrad, query_s, grad_s, key_t, factor,
    key, value, value_t, score,
):
    rows = slot_ref.shape[1]
    pieces, _, local, _ = own_ref.shape
    pre = pieces * local
    total = pre + rows
    chunks = total // CHUNK
    scale = 1.0 / math.sqrt(HD)
    log_scale = scale * math.log2(math.e)
    live = jnp.where(slot_ref[...] < BLOCK, 1.0, 0.0).astype(F32)

    for p in range(pieces):
        key[p * local : (p + 1) * local] = own_ref[p, 0] + other_ref[p, 0]
        value[p * local : (p + 1) * local] = own_ref[p, 1] + other_ref[p, 1]
    key[pre:] = rkey_ref[...]
    value[pre:] = rvalue_ref[...]

    def cut(k):
        return slice(k * CHUNK, (k + 1) * CHUNK)

    def at(g):
        return slice(g * rows, (g + 1) * rows)

    for k in range(chunks):
        key_t[:, cut(k)] = key[cut(k)].T
        value_t[:HD, cut(k)] = value[cut(k)].T
    value_t[HD:] = jnp.ones((value_t.shape[0] - HD, total), BF16)

    tops, dots = {}, {}

    def scores(g, k):
        s = nn(key[cut(k)], query[:, at(g)])
        if k == chunks - 1:
            s = s + rbias[...]
        else:
            b = bias[cut(k)]
            s = s + jnp.concatenate([b] * (rows // HD), axis=1)
        score[g % 2, cut(k)] = s
        top = jnp.max(s, axis=0, keepdims=True)
        tops[g] = top if k == 0 else jnp.maximum(tops[g], top)

    def weights(g, k):
        weight[cut(k), at(g)] = jnp.exp2((score[g % 2, cut(k)] - tops[g]) * log_scale).astype(BF16)

    def attend(g):
        both = nn(value_t[...], weight[:, at(g)])
        denom = both[HD : HD + 1]
        inverse = live / denom
        dots[g] = jnp.sum(both[:HD] * grad[:, at(g)].astype(F32), axis=0, keepdims=True) / denom
        factor[:, at(g)] = inverse * scale
        query_s[:, at(g)] = (query[:, at(g)].astype(F32) * (inverse * scale)).astype(BF16)
        grad_s[:, at(g)] = (grad[:, at(g)].astype(F32) * inverse).astype(BF16)

    def score_grads(g, k):
        d = nn(value[cut(k)], grad[:, at(g)])
        sgrad[cut(k), at(g)] = weight[cut(k), at(g)] * (d - dots[g]).astype(BF16)

    for t in range(GROUP + 2):
        for k in range(chunks):
            if t < GROUP:
                scores(t, k)
            if 1 <= t <= GROUP:
                weights(t - 1, k)
            if t >= 2:
                score_grads(t - 2, k)
        if 1 <= t <= GROUP:
            attend(t - 1)

    for k in range(pre // CHUNK):
        dk = nt(query_s[...], sgrad[cut(k)])
        dv = nt(grad_s[...], weight[cut(k)])
        for p in range(CHUNK // local):
            for n, d in enumerate((dk, dv)):
                part_ref[k * (CHUNK // local) + p, n] = d[:, p * local : (p + 1) * local].T.astype(BF16)


def response_kernel(weight, sgrad, query_s, grad_s, key_t, factor, dq_ref, drk_ref, drv_ref):
    rows = drk_ref.shape[0]
    pre = weight.shape[0] - rows
    drk_ref[...] = nt(query_s[...], sgrad[pre:]).T.astype(BF16)
    drv_ref[...] = nt(grad_s[...], weight[pre:]).T.astype(BF16)
    for g in range(GROUP):
        at = slice(g * rows, (g + 1) * rows)
        dq = nn(key_t[...], sgrad[:, at]) * factor[:, at]
        dq_ref[:, g * HD : (g + 1) * HD] = dq.T.astype(BF16)


def chip_sum_kernel(mine_ref, got_ref, out_ref):
    for h in range(KVH):
        block = (mine_ref[h].astype(F32) + got_ref[h].astype(F32)).astype(BF16)
        out_ref[h] = block
        out_ref[KVH + h] = block


def final_kernel(place_ref, got_ref, dk_ref, dv_ref):
    _, side, core = place()
    own = place_ref[0, 0] == side * 2 + core

    @pl.when(own)
    def _():
        for n, ref in enumerate((dk_ref, dv_ref)):
            for h in range(KVH):
                block = got_ref[h, n].astype(F32) + got_ref[KVH + h, n].astype(F32)
                ref[:, h * HD : (h + 1) * HD] = block.astype(BF16)

    @pl.when(jnp.logical_not(own))
    def _():
        for ref in (dk_ref, dv_ref):
            ref[...] = jnp.zeros_like(ref)


def on_device(
    queries,
    resp_keys,
    resp_values,
    out_grad,
    prefix_keys,
    prefix_values,
    resp_slot,
    prefix_len,
    prefix_owner,
):
    dp, heads = lax.axis_size("dp"), lax.axis_size("head")
    rows = queries.shape[0]
    local, width = prefix_keys.shape
    pre = local * heads
    total = pre + rows
    swap = [(d, d ^ 1) for d in range(dp)]
    groups = [
        [(base + 2 * side + core) * heads + h for side in range(2) for h in range(heads)]
        for base in range(0, dp, BLOCK)
        for core in range(2)
    ]

    def exchange(block):
        flat = block.reshape(2 * heads, 2 * local, HD)
        flat = lax.all_to_all(flat, ("dp", "head"), 0, 0, axis_index_groups=groups, tiled=True)
        return flat.reshape(block.shape)

    slot = resp_slot.reshape(1, rows)
    piece = (heads, 2, local, HD)
    both = (2 * heads, 2, local, HD)
    spread, flag, owner = call(
        spread_kernel,
        [struct(both, BF16), struct((1, 1), jnp.int32), struct((1, HD), jnp.int32)],
        prefix_owner.reshape(1, -1),
        prefix_keys,
        prefix_values,
        specs=[HBM, HBM, HBM],
        scratch=[
            pltpu.VMEM((2, local, width), BF16),
            pltpu.SMEM((1, prefix_owner.shape[0]), jnp.int32),
            pltpu.SemaphoreType.DMA((2 * PARTS + 1,)),
        ],
        vmem=60,
    )
    active = flag[0, 0] == 1
    arrived = lax.cond(active, exchange, jnp.zeros_like, spread)
    (own,) = call(side_kernel, [struct(piece, BF16)], arrived)
    other = lax.ppermute(own, "dp", swap)
    query_t, grad_t, bias, rbias = call(
        prepare_kernel,
        [
            struct((HD, GROUP * rows), BF16),
            struct((HD, GROUP * rows), BF16),
            struct((pre, HD), F32),
            struct((rows, rows), F32),
        ],
        prefix_len.reshape(1, -1),
        slot,
        queries,
        out_grad,
    )
    part, *saved = call(
        attention_kernel,
        [
            struct(piece, BF16),
            struct((total, GROUP * rows), BF16),
            struct((total, GROUP * rows), BF16),
            struct((HD, GROUP * rows), BF16),
            struct((HD, GROUP * rows), BF16),
            struct((HD, total), BF16),
            struct((1, GROUP * rows), F32),
        ],
        slot,
        query_t,
        grad_t,
        bias,
        rbias,
        own,
        other,
        resp_keys,
        resp_values,
        scratch=[
            pltpu.VMEM((total, HD), BF16),
            pltpu.VMEM((total, HD), BF16),
            pltpu.VMEM((HD + 16, total), BF16),
            pltpu.VMEM((2, total, rows), F32),
        ],
        flops=10 * GROUP * rows * total * HD,
    )
    got = lax.ppermute(part, "dp", swap)
    dq, drk, drv = call(
        response_kernel,
        [struct(queries.shape, BF16), struct(resp_keys.shape, BF16), struct(resp_values.shape, BF16)],
        *saved,
        flops=2 * GROUP * rows * total * HD,
    )
    (spread,) = call(chip_sum_kernel, [struct(both, BF16)], part, got)
    arrived = lax.cond(active, exchange, lambda block: block, spread)
    dk, dv = call(
        final_kernel,
        [struct(prefix_keys.shape, BF16), struct(prefix_values.shape, BF16)],
        owner,
        arrived,
    )
    return dq, drk, drv, dk, dv


def solution(mesh):
    placed = (
        P("dp", "head"),
        P("dp", "head"),
        P("dp", "head"),
        P("dp", "head"),
        P(("dp", "head"), None),
        P(("dp", "head"), None),
        P("dp"),
        P(),
        P(),
    )
    return jax.shard_map(
        on_device,
        mesh=mesh,
        in_specs=placed,
        out_specs=(
            P("dp", "head"),
            P("dp", "head"),
            P("dp", "head"),
            P(("dp", "head"), None),
            P(("dp", "head"), None),
        ),
        check_vma=False,
    )
```

```python
import math

import jax
import jax.numpy as jnp
from jax import lax
from jax.experimental import pallas as pl
from jax.experimental.pallas import tpu as pltpu
from jax.sharding import PartitionSpec as P

HD = 128
QH = 64
KVH = 8
BLOCK = 4
GROUP = QH // KVH
CHUNK = 256
MASKED = -1e30

F32 = jnp.float32
BF16 = jnp.bfloat16
VMEM = pl.BlockSpec(memory_space=pltpu.VMEM)
HBM = pl.BlockSpec(memory_space=pltpu.HBM)
MIB = 1024 * 1024
PARTS = 4


def place():
    index = lax.axis_index("dp")
    return index // BLOCK, (index % BLOCK) // 2, index % 2


def members(heads):
    low, ring = 2, heads // 2
    order = []
    for y in range(ring):
        line = [(x // low, x % low, y) for x in range(2 * low)]
        order += line if y % 2 == 0 else line[::-1]
    return [(side, x * ring + y) for side, x, y in order]


PLACE = {member: n for n, member in enumerate(members(KVH))}


def nt(a, b):
    return lax.dot_general(a, b, (((1,), (1,)), ((), ())), preferred_element_type=F32)


def nn(a, b):
    return jnp.dot(a, b, preferred_element_type=F32)


def call(kernel, outs, *args, specs=None, out_specs=None, scratch=(), flops=0, vmem=32):
    size = sum(math.prod(a.shape) * a.dtype.itemsize for a in list(args) + list(outs))
    return pl.pallas_call(
        kernel,
        out_shape=tuple(outs),
        in_specs=specs or [VMEM for _ in args],
        out_specs=tuple(out_specs or [VMEM for _ in outs]),
        scratch_shapes=list(scratch),
        compiler_params=pltpu.CompilerParams(vmem_limit_bytes=vmem * MIB),
        cost_estimate=pl.CostEstimate(flops=flops, bytes_accessed=size, transcendentals=0),
    )(*args)


def struct(shape, dtype):
    return jax.ShapeDtypeStruct(shape, dtype)


def spread_kernel(owner_ref, key_ref, value_ref, out_ref, flag_ref, place_ref, flag, spot, slots, owners, sems):
    first = pltpu.make_async_copy(owner_ref, owners, sems.at[0])
    first.start()
    copies = []
    for n, ref in enumerate((key_ref, value_ref)):
        for part in range(PARTS):
            rows = slice(part * HD // PARTS, (part + 1) * HD // PARTS)
            copies.append(pltpu.make_async_copy(ref.at[rows, :], slots.at[n, rows, :], sems.at[len(copies) + 1]))
    for copy in copies:
        copy.start()
    first.wait()
    prompt, side, core = place()
    owner = owners[0, prompt]
    flag[...] = jnp.full(flag.shape, (owner % 2 == core).astype(jnp.int32))
    spot[...] = jnp.full(spot.shape, owner)
    small = [
        pltpu.make_async_copy(flag, flag_ref, sems.at[2 * PARTS + 1]),
        pltpu.make_async_copy(spot, place_ref, sems.at[2 * PARTS + 2]),
    ]
    for copy in small:
        copy.start()

    @pl.when(owner // 2 != side)
    def _():
        out_ref[...] = jnp.zeros_like(out_ref)

    for n in range(2):
        for copy in copies[n * PARTS : (n + 1) * PARTS]:
            copy.wait()

        @pl.when(owner // 2 == side)
        def _():
            for h in range(KVH):
                block = slots[n, :, h * HD : (h + 1) * HD]
                out_ref[PLACE[0, h], n] = block
                out_ref[PLACE[1, h], n] = block

    for copy in small:
        copy.wait()


def side_kernel(got_ref, out_ref):
    for h in range(KVH):
        out_ref[h] = got_ref[PLACE[0, h]] + got_ref[PLACE[1, h]]


def prepare_kernel(
    len_ref, slot_ref, query_ref, grad_ref, rkey_ref, rvalue_ref, query_t, grad_t, bias, rscore, rdprod
):
    rows = query_ref.shape[0]
    for g in range(GROUP):
        at = slice(g * rows, (g + 1) * rows)
        lanes = slice(g * HD, (g + 1) * HD)
        query_t[:, at] = query_ref[:, lanes].T
        grad_t[:, at] = grad_ref[:, lanes].T
    prompt, _, _ = place()
    lane = lax.broadcasted_iota(jnp.int32, len_ref.shape, 1)
    count = jnp.sum(jnp.where(lane == prompt, len_ref[...], 0).astype(F32), axis=1, keepdims=True)
    column = lax.broadcasted_iota(jnp.int32, bias.shape, 0).astype(F32)
    bias[...] = jnp.where(column < count, 0.0, MASKED).astype(F32)
    slot_row = jnp.broadcast_to(slot_ref[...].astype(F32), (rows, rows))
    slot_col = slot_row.T
    at_key = lax.broadcasted_iota(jnp.int32, (rows, rows), 0)
    at_row = lax.broadcasted_iota(jnp.int32, (rows, rows), 1)
    seen = jnp.logical_and(slot_row == slot_col, at_key <= at_row)
    rbias = jnp.where(seen, 0.0, MASKED).astype(F32)
    for g in range(GROUP):
        at = slice(g * rows, (g + 1) * rows)
        rscore[:, at] = nn(rkey_ref[...], query_t[:, at]) + rbias
        rdprod[:, at] = nn(rvalue_ref[...], grad_t[:, at])


def attention_kernel(
    slot_ref, query, grad, bias, rscore, rdprod, own_ref, other_ref, rkey_ref, rvalue_ref,
    part_ref, weight, sgrad, query_s, grad_s, key_t, factor,
    key, value, value_t, score,
):
    rows = slot_ref.shape[1]
    pieces, _, local, _ = own_ref.shape
    pre = pieces * local
    total = pre + rows
    chunks = total // CHUNK
    scale = 1.0 / math.sqrt(HD)
    log_scale = scale * math.log2(math.e)
    live = jnp.where(slot_ref[...] < BLOCK, 1.0, 0.0).astype(F32)

    for p in range(pieces):
        key[p * local : (p + 1) * local] = own_ref[p, 0] + other_ref[p, 0]
        value[p * local : (p + 1) * local] = own_ref[p, 1] + other_ref[p, 1]
    key[pre:] = rkey_ref[...]
    value[pre:] = rvalue_ref[...]

    def cut(k):
        return slice(k * CHUNK, (k + 1) * CHUNK)

    def at(g):
        return slice(g * rows, (g + 1) * rows)

    for k in range(chunks):
        key_t[:, cut(k)] = key[cut(k)].T
        value_t[:HD, cut(k)] = value[cut(k)].T
    value_t[HD:] = jnp.ones((value_t.shape[0] - HD, total), BF16)

    tops, dots = {}, {}

    def scores(g, k):
        if k == chunks - 1:
            s = rscore[:, at(g)]
        else:
            b = bias[cut(k)]
            s = nn(key[cut(k)], query[:, at(g)]) + jnp.concatenate([b] * (rows // HD), axis=1)
            score[g % 2, cut(k)] = s
        top = jnp.max(s, axis=0, keepdims=True)
        tops[g] = top if k == 0 else jnp.maximum(tops[g], top)

    def weights(g, k):
        s = rscore[:, at(g)] if k == chunks - 1 else score[g % 2, cut(k)]
        weight[cut(k), at(g)] = jnp.exp2((s - tops[g]) * log_scale).astype(BF16)

    def attend(g):
        both = nn(value_t[...], weight[:, at(g)])
        denom = both[HD : HD + 1]
        inverse = live / denom
        dots[g] = jnp.sum(both[:HD] * grad[:, at(g)].astype(F32), axis=0, keepdims=True) / denom
        factor[:, at(g)] = inverse * scale
        query_s[:, at(g)] = (query[:, at(g)].astype(F32) * (inverse * scale)).astype(BF16)
        grad_s[:, at(g)] = (grad[:, at(g)].astype(F32) * inverse).astype(BF16)

    def score_grads(g, k):
        d = rdprod[:, at(g)] if k == chunks - 1 else nn(value[cut(k)], grad[:, at(g)])
        sgrad[cut(k), at(g)] = weight[cut(k), at(g)] * (d - dots[g]).astype(BF16)

    for t in range(GROUP + 2):
        for k in range(chunks):
            if t < GROUP:
                scores(t, k)
            if 1 <= t <= GROUP:
                weights(t - 1, k)
            if t >= 2:
                score_grads(t - 2, k)
        if 1 <= t <= GROUP:
            attend(t - 1)

    for k in range(pre // CHUNK):
        dk = nt(query_s[...], sgrad[cut(k)])
        dv = nt(grad_s[...], weight[cut(k)])
        for p in range(CHUNK // local):
            for n, d in enumerate((dk, dv)):
                part_ref[k * (CHUNK // local) + p, n] = d[:, p * local : (p + 1) * local].T.astype(BF16)


def response_kernel(weight, sgrad, query_s, grad_s, key_t, factor, dq_ref, drk_ref, drv_ref, dq, drk, drv, sems):
    rows = drk.shape[0]
    pre = weight.shape[0] - rows
    copies = []

    def leave(source, target):
        copies.append(pltpu.make_async_copy(source, target, sems.at[len(copies)]))
        copies[-1].start()

    for g in range(GROUP):
        at = slice(g * rows, (g + 1) * rows)
        lanes = slice(g * HD, (g + 1) * HD)
        dq[:, lanes] = (nn(key_t[...], sgrad[:, at]) * factor[:, at]).T.astype(BF16)
        leave(dq.at[:, lanes], dq_ref.at[:, lanes])
    drk[...] = nt(query_s[...], sgrad[pre:]).T.astype(BF16)
    leave(drk, drk_ref)
    drv[...] = nt(grad_s[...], weight[pre:]).T.astype(BF16)
    leave(drv, drv_ref)
    for copy in copies:
        copy.wait()


def chip_sum_kernel(mine_ref, got_ref, out_ref):
    for h in range(KVH):
        block = (mine_ref[h].astype(F32) + got_ref[h].astype(F32)).astype(BF16)
        out_ref[PLACE[0, h]] = block
        out_ref[PLACE[1, h]] = block


def final_kernel(place_ref, got_ref, dk_ref, dv_ref, sums, sems):
    _, side, core = place()
    own = place_ref[0, 0] == side * 2 + core
    half = sums.shape[1] // 2
    copies = []
    for n, ref in enumerate((dk_ref, dv_ref)):
        for part in range(2):
            rows = slice(part * half, (part + 1) * half)

            @pl.when(own)
            def _():
                for h in range(KVH):
                    block = got_ref[PLACE[0, h], n, rows].astype(F32) + got_ref[PLACE[1, h], n, rows].astype(F32)
                    sums[n, rows, h * HD : (h + 1) * HD] = block.astype(BF16)

            @pl.when(jnp.logical_not(own))
            def _():
                sums[n, rows] = jnp.zeros((half, sums.shape[2]), BF16)

            copies.append(pltpu.make_async_copy(sums.at[n, rows], ref.at[rows], sems.at[len(copies)]))
            copies[-1].start()
    for copy in copies:
        copy.wait()


def on_device(
    queries,
    resp_keys,
    resp_values,
    out_grad,
    prefix_keys,
    prefix_values,
    resp_slot,
    prefix_len,
    prefix_owner,
):
    dp, heads = lax.axis_size("dp"), lax.axis_size("head")
    rows = queries.shape[0]
    local, width = prefix_keys.shape
    pre = local * heads
    total = pre + rows
    swap = [(d, d ^ 1) for d in range(dp)]
    groups = [
        [(base + 2 * side + core) * heads + h for side, h in members(heads)]
        for base in range(0, dp, BLOCK)
        for core in range(2)
    ]

    def exchange(block):
        flat = block.reshape(2 * heads, 2 * local, HD)
        flat = lax.all_to_all(flat, ("dp", "head"), 0, 0, axis_index_groups=groups, tiled=True)
        return flat.reshape(block.shape)

    slot = resp_slot.reshape(1, rows)
    piece = (heads, 2, local, HD)
    both = (2 * heads, 2, local, HD)
    spread, flag, owner = call(
        spread_kernel,
        [struct(both, BF16), struct((1, 1), jnp.int32), struct((1, HD), jnp.int32)],
        prefix_owner.reshape(1, -1),
        prefix_keys,
        prefix_values,
        specs=[HBM, HBM, HBM],
        out_specs=[VMEM, HBM, HBM],
        scratch=[
            pltpu.VMEM((1, 1), jnp.int32),
            pltpu.VMEM((1, HD), jnp.int32),
            pltpu.VMEM((2, local, width), BF16),
            pltpu.SMEM((1, prefix_owner.shape[0]), jnp.int32),
            pltpu.SemaphoreType.DMA((2 * PARTS + 3,)),
        ],
        vmem=60,
    )
    active = flag[0, 0] == 1
    arrived = lax.cond(active, exchange, jnp.zeros_like, spread)
    (own,) = call(side_kernel, [struct(piece, BF16)], arrived)
    other = lax.ppermute(own, "dp", swap)
    query_t, grad_t, bias, rscore, rdprod = call(
        prepare_kernel,
        [
            struct((HD, GROUP * rows), BF16),
            struct((HD, GROUP * rows), BF16),
            struct((pre, HD), F32),
            struct((rows, GROUP * rows), F32),
            struct((rows, GROUP * rows), F32),
        ],
        prefix_len.reshape(1, -1),
        slot,
        queries,
        out_grad,
        resp_keys,
        resp_values,
    )
    part, *saved = call(
        attention_kernel,
        [
            struct(piece, BF16),
            struct((total, GROUP * rows), BF16),
            struct((total, GROUP * rows), BF16),
            struct((HD, GROUP * rows), BF16),
            struct((HD, GROUP * rows), BF16),
            struct((HD, total), BF16),
            struct((1, GROUP * rows), F32),
        ],
        slot,
        query_t,
        grad_t,
        bias,
        rscore,
        rdprod,
        own,
        other,
        resp_keys,
        resp_values,
        scratch=[
            pltpu.VMEM((total, HD), BF16),
            pltpu.VMEM((total, HD), BF16),
            pltpu.VMEM((HD + 16, total), BF16),
            pltpu.VMEM((2, pre, rows), F32),
        ],
        flops=10 * GROUP * rows * total * HD,
    )
    got = lax.ppermute(part, "dp", swap)
    dq, drk, drv = call(
        response_kernel,
        [struct(queries.shape, BF16), struct(resp_keys.shape, BF16), struct(resp_values.shape, BF16)],
        *saved,
        out_specs=[HBM, HBM, HBM],
        scratch=[
            pltpu.VMEM(queries.shape, BF16),
            pltpu.VMEM(resp_keys.shape, BF16),
            pltpu.VMEM(resp_values.shape, BF16),
            pltpu.SemaphoreType.DMA((GROUP + 2,)),
        ],
        flops=2 * GROUP * rows * total * HD,
    )
    (spread,) = call(chip_sum_kernel, [struct(both, BF16)], part, got)
    arrived = lax.cond(active, exchange, lambda block: block, spread)
    dk, dv = call(
        final_kernel,
        [struct(prefix_keys.shape, BF16), struct(prefix_values.shape, BF16)],
        owner,
        arrived,
        out_specs=[HBM, HBM],
        scratch=[pltpu.VMEM((2, local, width), BF16), pltpu.SemaphoreType.DMA((4,))],
    )
    return dq, drk, drv, dk, dv


def solution(mesh):
    placed = (
        P("dp", "head"),
        P("dp", "head"),
        P("dp", "head"),
        P("dp", "head"),
        P(("dp", "head"), None),
        P(("dp", "head"), None),
        P("dp"),
        P(),
        P(),
    )
    return jax.shard_map(
        on_device,
        mesh=mesh,
        in_specs=placed,
        out_specs=(
            P("dp", "head"),
            P("dp", "head"),
            P("dp", "head"),
            P(("dp", "head"), None),
            P(("dp", "head"), None),
        ),
        check_vma=False,
    )
```

```python
import math

import jax
import jax.numpy as jnp
from jax import lax
from jax.experimental import pallas as pl
from jax.experimental.pallas import tpu as pltpu
from jax.sharding import PartitionSpec as P

HD = 128
QH = 64
KVH = 8
BLOCK = 4
GROUP = QH // KVH
CHUNK = 512
SHORTEST = 512
MASKED = -1e30

F32 = jnp.float32
BF16 = jnp.bfloat16
VMEM = pl.BlockSpec(memory_space=pltpu.VMEM)
HBM = pl.BlockSpec(memory_space=pltpu.HBM)
MIB = 1024 * 1024
PARTS = 4


def place():
    index = lax.axis_index("dp")
    return index // BLOCK, (index % BLOCK) // 2, index % 2


def members(heads):
    low, ring = 2, heads // 2
    order = []
    for y in range(ring):
        line = [(x // low, x % low, y) for x in range(2 * low)]
        order += line if y % 2 == 0 else line[::-1]
    return [(side, x * ring + y) for side, x, y in order]


PLACE = {member: n for n, member in enumerate(members(KVH))}


def nn(a, b):
    return jnp.dot(a, b, preferred_element_type=F32)


def call(kernel, outs, *args, specs=None, out_specs=None, scratch=(), flops=0, vmem=32):
    size = sum(math.prod(a.shape) * a.dtype.itemsize for a in list(args) + list(outs))
    return pl.pallas_call(
        kernel,
        out_shape=tuple(outs),
        in_specs=specs or [VMEM for _ in args],
        out_specs=tuple(out_specs or [VMEM for _ in outs]),
        scratch_shapes=list(scratch),
        compiler_params=pltpu.CompilerParams(vmem_limit_bytes=vmem * MIB),
        cost_estimate=pl.CostEstimate(flops=flops, bytes_accessed=size, transcendentals=0),
    )(*args)


def struct(shape, dtype):
    return jax.ShapeDtypeStruct(shape, dtype)


def spread_kernel(owner_ref, key_ref, value_ref, out_ref, flag_ref, place_ref, flag, spot, slots, owners, sems):
    first = pltpu.make_async_copy(owner_ref, owners, sems.at[0])
    first.start()
    copies = []
    for n, ref in enumerate((key_ref, value_ref)):
        for part in range(PARTS):
            rows = slice(part * HD // PARTS, (part + 1) * HD // PARTS)
            copies.append(pltpu.make_async_copy(ref.at[rows, :], slots.at[n, rows, :], sems.at[len(copies) + 1]))
    for copy in copies:
        copy.start()
    first.wait()
    prompt, side, core = place()
    owner = owners[0, prompt]
    flag[...] = jnp.full(flag.shape, (owner % 2 == core).astype(jnp.int32))
    spot[...] = jnp.full(spot.shape, owner)
    small = [
        pltpu.make_async_copy(flag, flag_ref, sems.at[2 * PARTS + 1]),
        pltpu.make_async_copy(spot, place_ref, sems.at[2 * PARTS + 2]),
    ]
    for copy in small:
        copy.start()

    @pl.when(owner // 2 != side)
    def _():
        out_ref[...] = jnp.zeros_like(out_ref)

    for n in range(2):
        for copy in copies[n * PARTS : (n + 1) * PARTS]:
            copy.wait()

        @pl.when(owner // 2 == side)
        def _():
            for h in range(KVH):
                block = slots[n, :, h * HD : (h + 1) * HD]
                out_ref[PLACE[0, h], n] = block
                out_ref[PLACE[1, h], n] = block

    for copy in small:
        copy.wait()


def side_kernel(got_ref, out_ref):
    for h in range(KVH):
        out_ref[h] = got_ref[PLACE[0, h]] + got_ref[PLACE[1, h]]


def prepare_kernel(
    len_ref, slot_ref, query_ref, grad_ref, rkey_ref, rvalue_ref, query_t, grad_t, bias, rscore, rdprod
):
    rows = query_ref.shape[0]
    for g in range(GROUP):
        at = slice(g * rows, (g + 1) * rows)
        lanes = slice(g * HD, (g + 1) * HD)
        query_t[:, at] = query_ref[:, lanes].T
        grad_t[:, at] = grad_ref[:, lanes].T
    prompt, _, _ = place()
    lane = lax.broadcasted_iota(jnp.int32, len_ref.shape, 1)
    count = jnp.sum(jnp.where(lane == prompt, len_ref[...], 0).astype(F32), axis=1, keepdims=True)
    column = lax.broadcasted_iota(jnp.int32, bias.shape, 0).astype(F32)
    bias[...] = jnp.where(column < count, 0.0, MASKED).astype(F32)
    slot_row = jnp.broadcast_to(slot_ref[...].astype(F32), (rows, rows))
    slot_col = slot_row.T
    at_key = lax.broadcasted_iota(jnp.int32, (rows, rows), 0)
    at_row = lax.broadcasted_iota(jnp.int32, (rows, rows), 1)
    seen = jnp.logical_and(slot_row == slot_col, at_key <= at_row)
    rbias = jnp.where(seen, 0.0, MASKED).astype(F32)
    for g in range(GROUP):
        at = slice(g * rows, (g + 1) * rows)
        rscore[:, at] = nn(rkey_ref[...], query_t[:, at]) + rbias
        rdprod[:, at] = nn(rvalue_ref[...], grad_t[:, at])


def attention_kernel(
    slot_ref, query, grad, bias, rscore, rdprod, own_ref, other_ref, rkey_ref, rvalue_ref,
    part_ref, weight, sgrad, query_s, grad_s, key_t, factor,
    key, value, value_t, score,
):
    rows = slot_ref.shape[1]
    pieces, _, local, _ = own_ref.shape
    pre = pieces * local
    total = pre + rows
    chunks, ahead = pre // CHUNK + 1, pre // CHUNK
    scale = 1.0 / math.sqrt(HD)
    log_scale = scale * math.log2(math.e)
    live = jnp.where(slot_ref[...] < BLOCK, 1.0, 0.0).astype(F32)

    for p in range(pieces):
        key[p * local : (p + 1) * local] = own_ref[p, 0] + other_ref[p, 0]
        value[p * local : (p + 1) * local] = own_ref[p, 1] + other_ref[p, 1]
    key[pre:] = rkey_ref[...]
    value[pre:] = rvalue_ref[...]

    cuts = [slice(a, a + CHUNK) for a in range(0, pre, CHUNK)] + [slice(pre, total)]

    def cut(k):
        return cuts[k]

    def at(g):
        return slice(g * rows, (g + 1) * rows)

    for k in range(chunks):
        key_t[:, cut(k)] = key[cut(k)].T
        value_t[:HD, cut(k)] = value[cut(k)].T
    value_t[HD:] = jnp.ones((value_t.shape[0] - HD, total), BF16)

    tops, dots = {}, {}

    def scores(g, k):
        if k >= ahead:
            s = rscore[:, at(g)]
        else:
            s = nn(key[cut(k)], query[:, at(g)])
            if cuts[k].stop > SHORTEST:
                s = s + jnp.concatenate([bias[cut(k)]] * (rows // HD), axis=1)
            score[g % 2, cut(k)] = s
        top = jnp.max(s, axis=0, keepdims=True)
        tops[g] = top if k == 0 else jnp.maximum(tops[g], top)

    def weights(g, k):
        s = rscore[:, at(g)] if k >= ahead else score[g % 2, cut(k)]
        weight[cut(k), at(g)] = jnp.exp2((s - tops[g]) * log_scale).astype(BF16)

    def attend(g):
        both = nn(value_t[...], weight[:, at(g)])
        denom = both[HD : HD + 1]
        inverse = live / denom
        dots[g] = jnp.sum(both[:HD] * grad[:, at(g)].astype(F32), axis=0, keepdims=True) / denom
        factor[:, at(g)] = inverse * scale
        query_s[at(g)] = (query[:, at(g)].astype(F32) * (inverse * scale)).astype(BF16).T
        grad_s[at(g)] = (grad[:, at(g)].astype(F32) * inverse).astype(BF16).T

    def score_grads(g, k):
        d = rdprod[:, at(g)] if k >= ahead else nn(value[cut(k)], grad[:, at(g)])
        sgrad[cut(k), at(g)] = weight[cut(k), at(g)] * (d - dots[g]).astype(BF16)

    for t in range(GROUP + 2):
        for k in range(chunks):
            if t < GROUP:
                scores(t, k)
            if 1 <= t <= GROUP:
                weights(t - 1, k)
            if t >= 2:
                score_grads(t - 2, k)
        if 1 <= t <= GROUP:
            attend(t - 1)

    for k in range(ahead):
        for n, d in enumerate((nn(sgrad[cut(k)], query_s[...]), nn(weight[cut(k)], grad_s[...]))):
            for p in range(CHUNK // local):
                part_ref[k * (CHUNK // local) + p, n] = d[p * local : (p + 1) * local].astype(BF16)


def response_kernel(weight, sgrad, query_s, grad_s, key_t, factor, dq_ref, drk_ref, drv_ref):
    rows = drk_ref.shape[0]
    pre = weight.shape[0] - rows
    drk_ref[...] = nn(sgrad[pre:], query_s[...]).astype(BF16)
    drv_ref[...] = nn(weight[pre:], grad_s[...]).astype(BF16)
    for g in range(GROUP):
        at = slice(g * rows, (g + 1) * rows)
        dq_ref[:, g * HD : (g + 1) * HD] = (nn(key_t[...], sgrad[:, at]) * factor[:, at]).T.astype(BF16)


def chip_sum_kernel(mine_ref, got_ref, out_ref):
    for h in range(KVH):
        block = (mine_ref[h].astype(F32) + got_ref[h].astype(F32)).astype(BF16)
        out_ref[PLACE[0, h]] = block
        out_ref[PLACE[1, h]] = block


def final_kernel(
    place_ref, got_ref, dq, drk, drv, dq_ref, drk_ref, drv_ref, dk_ref, dv_ref, sums, sems
):
    _, side, core = place()
    own = place_ref[0, 0] == side * 2 + core
    half = sums.shape[1] // 2
    copies = [
        pltpu.make_async_copy(dq, dq_ref, sems.at[0]),
        pltpu.make_async_copy(drk, drk_ref, sems.at[1]),
        pltpu.make_async_copy(drv, drv_ref, sems.at[2]),
    ]
    for copy in copies:
        copy.start()
    for n, ref in enumerate((dk_ref, dv_ref)):
        for part in range(2):
            rows = slice(part * half, (part + 1) * half)

            @pl.when(own)
            def _():
                for h in range(KVH):
                    block = got_ref[PLACE[0, h], n, rows].astype(F32) + got_ref[PLACE[1, h], n, rows].astype(F32)
                    sums[n, rows, h * HD : (h + 1) * HD] = block.astype(BF16)

            @pl.when(jnp.logical_not(own))
            def _():
                sums[n, rows] = jnp.zeros((half, sums.shape[2]), BF16)

            copies.append(pltpu.make_async_copy(sums.at[n, rows], ref.at[rows], sems.at[len(copies)]))
            copies[-1].start()
    for copy in copies:
        copy.wait()


def on_device(
    queries,
    resp_keys,
    resp_values,
    out_grad,
    prefix_keys,
    prefix_values,
    resp_slot,
    prefix_len,
    prefix_owner,
):
    dp, heads = lax.axis_size("dp"), lax.axis_size("head")
    rows = queries.shape[0]
    local, width = prefix_keys.shape
    pre = local * heads
    total = pre + rows
    swap = [(d, d ^ 1) for d in range(dp)]
    groups = [
        [(base + 2 * side + core) * heads + h for side, h in members(heads)]
        for base in range(0, dp, BLOCK)
        for core in range(2)
    ]

    def exchange(block):
        flat = block.reshape(2 * heads, 2 * local, HD)
        flat = lax.all_to_all(flat, ("dp", "head"), 0, 0, axis_index_groups=groups, tiled=True)
        return flat.reshape(block.shape)

    slot = resp_slot.reshape(1, rows)
    piece = (heads, 2, local, HD)
    both = (2 * heads, 2, local, HD)
    spread, flag, owner = call(
        spread_kernel,
        [struct(both, BF16), struct((1, 1), jnp.int32), struct((1, HD), jnp.int32)],
        prefix_owner.reshape(1, -1),
        prefix_keys,
        prefix_values,
        specs=[HBM, HBM, HBM],
        out_specs=[VMEM, HBM, HBM],
        scratch=[
            pltpu.VMEM((1, 1), jnp.int32),
            pltpu.VMEM((1, HD), jnp.int32),
            pltpu.VMEM((2, local, width), BF16),
            pltpu.SMEM((1, prefix_owner.shape[0]), jnp.int32),
            pltpu.SemaphoreType.DMA((2 * PARTS + 3,)),
        ],
        vmem=60,
    )
    active = flag[0, 0] == 1
    arrived = lax.cond(active, exchange, jnp.zeros_like, spread)
    (own,) = call(side_kernel, [struct(piece, BF16)], arrived)
    other = lax.ppermute(own, "dp", swap)
    query_t, grad_t, bias, rscore, rdprod = call(
        prepare_kernel,
        [
            struct((HD, GROUP * rows), BF16),
            struct((HD, GROUP * rows), BF16),
            struct((pre, HD), F32),
            struct((rows, GROUP * rows), F32),
            struct((rows, GROUP * rows), F32),
        ],
        prefix_len.reshape(1, -1),
        slot,
        queries,
        out_grad,
        resp_keys,
        resp_values,
    )
    part, *saved = call(
        attention_kernel,
        [
            struct(piece, BF16),
            struct((total, GROUP * rows), BF16),
            struct((total, GROUP * rows), BF16),
            struct((GROUP * rows, HD), BF16),
            struct((GROUP * rows, HD), BF16),
            struct((HD, total), BF16),
            struct((1, GROUP * rows), F32),
        ],
        slot,
        query_t,
        grad_t,
        bias,
        rscore,
        rdprod,
        own,
        other,
        resp_keys,
        resp_values,
        scratch=[
            pltpu.VMEM((total, HD), BF16),
            pltpu.VMEM((total, HD), BF16),
            pltpu.VMEM((HD + 16, total), BF16),
            pltpu.VMEM((2, pre, rows), F32),
        ],
        flops=10 * GROUP * rows * total * HD,
    )
    got = lax.ppermute(part, "dp", swap)
    dq, drk, drv = call(
        response_kernel,
        [struct(queries.shape, BF16), struct(resp_keys.shape, BF16), struct(resp_values.shape, BF16)],
        *saved,
        flops=2 * GROUP * rows * total * HD,
    )
    (spread,) = call(chip_sum_kernel, [struct(both, BF16)], part, got)
    arrived = lax.cond(active, exchange, lambda block: block, spread)
    return call(
        final_kernel,
        [
            struct(queries.shape, BF16),
            struct(resp_keys.shape, BF16),
            struct(resp_values.shape, BF16),
            struct(prefix_keys.shape, BF16),
            struct(prefix_values.shape, BF16),
        ],
        owner,
        arrived,
        dq,
        drk,
        drv,
        out_specs=[HBM] * 5,
        scratch=[pltpu.VMEM((2, local, width), BF16), pltpu.SemaphoreType.DMA((7,))],
    )


def solution(mesh):
    placed = (
        P("dp", "head"),
        P("dp", "head"),
        P("dp", "head"),
        P("dp", "head"),
        P(("dp", "head"), None),
        P(("dp", "head"), None),
        P("dp"),
        P(),
        P(),
    )
    return jax.shard_map(
        on_device,
        mesh=mesh,
        in_specs=placed,
        out_specs=(
            P("dp", "head"),
            P("dp", "head"),
            P("dp", "head"),
            P(("dp", "head"), None),
            P(("dp", "head"), None),
        ),
        check_vma=False,
    )
```

```python
import math

import jax
import jax.numpy as jnp
from jax import lax
from jax.experimental import pallas as pl
from jax.experimental.pallas import tpu as pltpu
from jax.sharding import PartitionSpec as P

HD = 128
QH = 64
KVH = 8
BLOCK = 4
GROUP = QH // KVH
CHUNK = 512
SHORTEST = 512
MASKED = -1e30

F32 = jnp.float32
BF16 = jnp.bfloat16
VMEM = pl.BlockSpec(memory_space=pltpu.VMEM)
HBM = pl.BlockSpec(memory_space=pltpu.HBM)
MIB = 1024 * 1024
PARTS = 4


def place():
    index = lax.axis_index("dp")
    return index // BLOCK, (index % BLOCK) // 2, index % 2


def members(heads):
    low, ring = 2, heads // 2
    order = []
    for y in range(ring):
        line = [(x // low, x % low, y) for x in range(2 * low)]
        order += line if y % 2 == 0 else line[::-1]
    return [(side, x * ring + y) for side, x, y in order]


PLACE = {member: n for n, member in enumerate(members(KVH))}


def nn(a, b):
    return jnp.dot(a, b, preferred_element_type=F32)


def call(kernel, outs, *args, specs=None, out_specs=None, scratch=(), flops=0, vmem=32):
    size = sum(math.prod(a.shape) * a.dtype.itemsize for a in list(args) + list(outs))
    return pl.pallas_call(
        kernel,
        out_shape=tuple(outs),
        in_specs=specs or [VMEM for _ in args],
        out_specs=tuple(out_specs or [VMEM for _ in outs]),
        scratch_shapes=list(scratch),
        compiler_params=pltpu.CompilerParams(vmem_limit_bytes=vmem * MIB),
        cost_estimate=pl.CostEstimate(flops=flops, bytes_accessed=size, transcendentals=0),
    )(*args)


def struct(shape, dtype):
    return jax.ShapeDtypeStruct(shape, dtype)


def spread_kernel(owner_ref, key_ref, value_ref, out_ref, flag_ref, place_ref, flag, spot, slots, owners, sems):
    first = pltpu.make_async_copy(owner_ref, owners, sems.at[0])
    first.start()
    copies = []
    for n, ref in enumerate((key_ref, value_ref)):
        for part in range(PARTS):
            rows = slice(part * HD // PARTS, (part + 1) * HD // PARTS)
            copies.append(pltpu.make_async_copy(ref.at[rows, :], slots.at[n, rows, :], sems.at[len(copies) + 1]))
    for copy in copies:
        copy.start()
    first.wait()
    prompt, side, core = place()
    owner = owners[0, prompt]
    flag[...] = jnp.full(flag.shape, (owner % 2 == core).astype(jnp.int32))
    spot[...] = jnp.full(spot.shape, owner)
    small = [
        pltpu.make_async_copy(flag, flag_ref, sems.at[2 * PARTS + 1]),
        pltpu.make_async_copy(spot, place_ref, sems.at[2 * PARTS + 2]),
    ]
    for copy in small:
        copy.start()

    @pl.when(owner // 2 != side)
    def _():
        out_ref[...] = jnp.zeros_like(out_ref)

    for n in range(2):
        for copy in copies[n * PARTS : (n + 1) * PARTS]:
            copy.wait()

        @pl.when(owner // 2 == side)
        def _():
            for h in range(KVH):
                block = slots[n, :, h * HD : (h + 1) * HD]
                out_ref[PLACE[0, h], n] = block
                out_ref[PLACE[1, h], n] = block

    for copy in small:
        copy.wait()


def side_kernel(got_ref, out_ref):
    for h in range(KVH):
        out_ref[h] = got_ref[PLACE[0, h]] + got_ref[PLACE[1, h]]


def prepare_kernel(
    len_ref, slot_ref, query_ref, grad_ref, rkey_ref, rvalue_ref, query_t, grad_t, bias, rscore, rdprod
):
    rows = query_ref.shape[0]
    for g in range(GROUP):
        at = slice(g * rows, (g + 1) * rows)
        lanes = slice(g * HD, (g + 1) * HD)
        query_t[:, at] = query_ref[:, lanes].T
        grad_t[:, at] = grad_ref[:, lanes].T
    prompt, _, _ = place()
    lane = lax.broadcasted_iota(jnp.int32, len_ref.shape, 1)
    count = jnp.sum(jnp.where(lane == prompt, len_ref[...], 0).astype(F32), axis=1, keepdims=True)
    column = lax.broadcasted_iota(jnp.int32, bias.shape, 0).astype(F32)
    bias[...] = jnp.where(column < count, 0.0, MASKED).astype(F32)
    slot_row = jnp.broadcast_to(slot_ref[...].astype(F32), (rows, rows))
    slot_col = slot_row.T
    at_key = lax.broadcasted_iota(jnp.int32, (rows, rows), 0)
    at_row = lax.broadcasted_iota(jnp.int32, (rows, rows), 1)
    seen = jnp.logical_and(slot_row == slot_col, at_key <= at_row)
    rbias = jnp.where(seen, 0.0, MASKED).astype(F32)
    for g in range(GROUP):
        at = slice(g * rows, (g + 1) * rows)
        rscore[:, at] = nn(rkey_ref[...], query_t[:, at]) + rbias
        rdprod[:, at] = nn(rvalue_ref[...], grad_t[:, at])


def attention_kernel(
    slot_ref, query, grad, bias, rscore, rdprod, own_ref, other_ref, rkey_ref, rvalue_ref,
    part_ref, rweight, sgrad, query_s, grad_s, key_t, factor,
    key, value, value_t, score, weight,
):
    rows = slot_ref.shape[1]
    pieces, _, local, _ = own_ref.shape
    pre = pieces * local
    total = pre + rows
    chunks, ahead = pre // CHUNK + 1, pre // CHUNK
    scale = 1.0 / math.sqrt(HD)
    log_scale = scale * math.log2(math.e)
    live = jnp.where(slot_ref[...] < BLOCK, 1.0, 0.0).astype(F32)

    for p in range(pieces):
        key[p * local : (p + 1) * local] = own_ref[p, 0] + other_ref[p, 0]
        value[p * local : (p + 1) * local] = own_ref[p, 1] + other_ref[p, 1]
    key[pre:] = rkey_ref[...]
    value[pre:] = rvalue_ref[...]

    cuts = [slice(a, a + CHUNK) for a in range(0, pre, CHUNK)] + [slice(pre, total)]

    def cut(k):
        return cuts[k]

    def at(g):
        return slice(g * rows, (g + 1) * rows)

    for k in range(chunks):
        key_t[:, cut(k)] = key[cut(k)].T
        value_t[:HD, cut(k)] = value[cut(k)].T
    value_t[HD:] = jnp.ones((value_t.shape[0] - HD, total), BF16)

    tops, dots = {}, {}

    def scores(g, k):
        if k >= ahead:
            s = rscore[:, at(g)]
        else:
            s = nn(key[cut(k)], query[:, at(g)])
            if cuts[k].stop > SHORTEST:
                s = s + jnp.concatenate([bias[cut(k)]] * (rows // HD), axis=1)
            score[g % 2, cut(k)] = s
        top = jnp.max(s, axis=0, keepdims=True)
        tops[g] = top if k == 0 else jnp.maximum(tops[g], top)

    def weights(g, k):
        s = rscore[:, at(g)] if k >= ahead else score[g % 2, cut(k)]
        e = jnp.exp2((s - tops[g]) * log_scale).astype(BF16)
        weight[cut(k), at(g)] = e
        if k >= ahead:
            rweight[:, at(g)] = e

    def attend(g):
        both = nn(value_t[...], weight[:, at(g)])
        denom = both[HD : HD + 1]
        inverse = live / denom
        dots[g] = jnp.sum(both[:HD] * grad[:, at(g)].astype(F32), axis=0, keepdims=True) / denom
        factor[:, at(g)] = inverse * scale
        query_s[at(g)] = (query[:, at(g)].astype(F32) * (inverse * scale)).astype(BF16).T
        grad_s[at(g)] = (grad[:, at(g)].astype(F32) * inverse).astype(BF16).T

    def score_grads(g, k):
        d = rdprod[:, at(g)] if k >= ahead else nn(value[cut(k)], grad[:, at(g)])
        sgrad[cut(k), at(g)] = weight[cut(k), at(g)] * (d - dots[g]).astype(BF16)

    for t in range(GROUP + 2):
        for k in range(chunks):
            if t < GROUP:
                scores(t, k)
            if 1 <= t <= GROUP:
                weights(t - 1, k)
            if t >= 2:
                score_grads(t - 2, k)
        if 1 <= t <= GROUP:
            attend(t - 1)

    for k in range(ahead):
        for n, d in enumerate((nn(sgrad[cut(k)], query_s[...]), nn(weight[cut(k)], grad_s[...]))):
            for p in range(CHUNK // local):
                part_ref[k * (CHUNK // local) + p, n] = d[p * local : (p + 1) * local].astype(BF16)


def response_kernel(rweight, sgrad, query_s, grad_s, key_t, factor, dq_ref, drk_ref, drv_ref):
    rows = drk_ref.shape[0]
    pre = sgrad.shape[0] - rows
    drk_ref[...] = nn(sgrad[pre:], query_s[...]).astype(BF16)
    drv_ref[...] = nn(rweight[...], grad_s[...]).astype(BF16)
    for g in range(GROUP):
        at = slice(g * rows, (g + 1) * rows)
        dq_ref[:, g * HD : (g + 1) * HD] = (nn(key_t[...], sgrad[:, at]) * factor[:, at]).T.astype(BF16)


def chip_sum_kernel(mine_ref, got_ref, out_ref):
    for h in range(KVH):
        block = (mine_ref[h].astype(F32) + got_ref[h].astype(F32)).astype(BF16)
        out_ref[PLACE[0, h]] = block
        out_ref[PLACE[1, h]] = block


def final_kernel(
    place_ref, got_ref, dq, drk, drv, dq_ref, drk_ref, drv_ref, dk_ref, dv_ref, sums, sems
):
    _, side, core = place()
    own = place_ref[0, 0] == side * 2 + core
    half = sums.shape[1] // 2
    copies = [
        pltpu.make_async_copy(dq, dq_ref, sems.at[0]),
        pltpu.make_async_copy(drk, drk_ref, sems.at[1]),
        pltpu.make_async_copy(drv, drv_ref, sems.at[2]),
    ]
    for copy in copies:
        copy.start()
    for n, ref in enumerate((dk_ref, dv_ref)):
        for part in range(2):
            rows = slice(part * half, (part + 1) * half)

            @pl.when(own)
            def _():
                for h in range(KVH):
                    block = got_ref[PLACE[0, h], n, rows].astype(F32) + got_ref[PLACE[1, h], n, rows].astype(F32)
                    sums[n, rows, h * HD : (h + 1) * HD] = block.astype(BF16)

            @pl.when(jnp.logical_not(own))
            def _():
                sums[n, rows] = jnp.zeros((half, sums.shape[2]), BF16)

            copies.append(pltpu.make_async_copy(sums.at[n, rows], ref.at[rows], sems.at[len(copies)]))
            copies[-1].start()
    for copy in copies:
        copy.wait()


def on_device(
    queries,
    resp_keys,
    resp_values,
    out_grad,
    prefix_keys,
    prefix_values,
    resp_slot,
    prefix_len,
    prefix_owner,
):
    dp, heads = lax.axis_size("dp"), lax.axis_size("head")
    rows = queries.shape[0]
    local, width = prefix_keys.shape
    pre = local * heads
    total = pre + rows
    swap = [(d, d ^ 1) for d in range(dp)]
    groups = [
        [(base + 2 * side + core) * heads + h for side, h in members(heads)]
        for base in range(0, dp, BLOCK)
        for core in range(2)
    ]

    def exchange(block):
        flat = block.reshape(2 * heads, 2 * local, HD)
        flat = lax.all_to_all(flat, ("dp", "head"), 0, 0, axis_index_groups=groups, tiled=True)
        return flat.reshape(block.shape)

    slot = resp_slot.reshape(1, rows)
    piece = (heads, 2, local, HD)
    both = (2 * heads, 2, local, HD)
    spread, flag, owner = call(
        spread_kernel,
        [struct(both, BF16), struct((1, 1), jnp.int32), struct((1, HD), jnp.int32)],
        prefix_owner.reshape(1, -1),
        prefix_keys,
        prefix_values,
        specs=[HBM, HBM, HBM],
        out_specs=[VMEM, HBM, HBM],
        scratch=[
            pltpu.VMEM((1, 1), jnp.int32),
            pltpu.VMEM((1, HD), jnp.int32),
            pltpu.VMEM((2, local, width), BF16),
            pltpu.SMEM((1, prefix_owner.shape[0]), jnp.int32),
            pltpu.SemaphoreType.DMA((2 * PARTS + 3,)),
        ],
        vmem=60,
    )
    active = flag[0, 0] == 1
    arrived = lax.cond(active, exchange, jnp.zeros_like, spread)
    (own,) = call(side_kernel, [struct(piece, BF16)], arrived)
    other = lax.ppermute(own, "dp", swap)
    query_t, grad_t, bias, rscore, rdprod = call(
        prepare_kernel,
        [
            struct((HD, GROUP * rows), BF16),
            struct((HD, GROUP * rows), BF16),
            struct((pre, HD), F32),
            struct((rows, GROUP * rows), F32),
            struct((rows, GROUP * rows), F32),
        ],
        prefix_len.reshape(1, -1),
        slot,
        queries,
        out_grad,
        resp_keys,
        resp_values,
    )
    part, *saved = call(
        attention_kernel,
        [
            struct(piece, BF16),
            struct((rows, GROUP * rows), BF16),
            struct((total, GROUP * rows), BF16),
            struct((GROUP * rows, HD), BF16),
            struct((GROUP * rows, HD), BF16),
            struct((HD, total), BF16),
            struct((1, GROUP * rows), F32),
        ],
        slot,
        query_t,
        grad_t,
        bias,
        rscore,
        rdprod,
        own,
        other,
        resp_keys,
        resp_values,
        scratch=[
            pltpu.VMEM((total, HD), BF16),
            pltpu.VMEM((total, HD), BF16),
            pltpu.VMEM((HD + 16, total), BF16),
            pltpu.VMEM((2, pre, rows), F32),
            pltpu.VMEM((total, GROUP * rows), BF16),
        ],
        flops=10 * GROUP * rows * total * HD,
    )
    got = lax.ppermute(part, "dp", swap)
    dq, drk, drv = call(
        response_kernel,
        [struct(queries.shape, BF16), struct(resp_keys.shape, BF16), struct(resp_values.shape, BF16)],
        *saved,
        flops=2 * GROUP * rows * total * HD,
    )
    (spread,) = call(chip_sum_kernel, [struct(both, BF16)], part, got)
    arrived = lax.cond(active, exchange, jnp.zeros_like, spread)
    return call(
        final_kernel,
        [
            struct(queries.shape, BF16),
            struct(resp_keys.shape, BF16),
            struct(resp_values.shape, BF16),
            struct(prefix_keys.shape, BF16),
            struct(prefix_values.shape, BF16),
        ],
        owner,
        arrived,
        dq,
        drk,
        drv,
        out_specs=[HBM] * 5,
        scratch=[pltpu.VMEM((2, local, width), BF16), pltpu.SemaphoreType.DMA((7,))],
    )


def solution(mesh):
    placed = (
        P("dp", "head"),
        P("dp", "head"),
        P("dp", "head"),
        P("dp", "head"),
        P(("dp", "head"), None),
        P(("dp", "head"), None),
        P("dp"),
        P(),
        P(),
    )
    return jax.shard_map(
        on_device,
        mesh=mesh,
        in_specs=placed,
        out_specs=(
            P("dp", "head"),
            P("dp", "head"),
            P("dp", "head"),
            P(("dp", "head"), None),
            P(("dp", "head"), None),
        ),
        check_vma=False,
    )
```
